32 devices in a mesh: chan: 16 (over z, y, core), tm: 2 (over x).
Axes of the slice: x: 2, y: 2, z: 4, core: 2. Of those that a mesh axis runs over, the one named last changes fastest.
Arguments:
- traces: bfloat16 [16, 48, 128, 1024], P('chan', 'tm'), may hold values from -6 to 6
- valid_mask: int32 [16, 48, 1024], P('chan', 'tm'), may hold values 0 or 1
- pair_owner: int32 [16, 4], P('chan'), may hold values from -1 to 15, as said below
Outputs:
- correlations: float32 [16, 4, 101, 128], P('chan')
The draws below stay inside these ranges and needn't reach their ends.
Inputs may be any that keep to these rules, and one draw needn't show every extreme that they name: `pair_owner`: row r lists distinct owners in r + 1 .. r + 4 (within the cable) in its leading slots, then -1; every reader with a block above it has one pair or more, and reader 0 fills all 4 slots.
All inputs are finite; a program needn't handle non-finite values. No bound on the sum of `valid_mask` on one device may be relied on, other than what follows from the above.
Results may differ from the reference program's by a relative error of at most 0.0052.
Values may be sent and summed in bfloat16 or wider, within the bound.
A program may use at most 64 MiB of HBM per device.

```python
import math
import jax
import jax.numpy as jnp
from jax import lax

BLOCK = 128
WIN = 1024
NF = 256
MAXLAG = 50
SMOOTH = 4
REACH = 4
BLOCKS = 16
WINDOWS = 48
LAGS = 101


def draw_pair_owner(key, part):
    key_order, key_count = jax.random.split(jax.random.fold_in(key, 11))
    reader = jnp.arange(BLOCKS, dtype=jnp.int32)[:, None]
    steps = jnp.arange(1, REACH + 1, dtype=jnp.int32)[None, :]
    inside = reader + steps < BLOCKS
    scores = jax.random.randint(key_order, (BLOCKS, REACH), 0, 1 << 16, dtype=jnp.int32) * REACH + (steps - 1)
    biggest = (1 << 16) * REACH + REACH
    scores = jnp.where(inside, scores, biggest)
    order = jnp.argsort(scores, axis=1, stable=True)
    picked = jnp.take_along_axis(jnp.broadcast_to(steps, (BLOCKS, REACH)), order, axis=1)
    available = jnp.sum(inside.astype(jnp.int32), axis=1)
    counts = jax.random.randint(key_count, (BLOCKS,), 1, REACH + 1, dtype=jnp.int32)
    counts = jnp.where(jnp.arange(BLOCKS, dtype=jnp.int32) == 0, REACH, counts)
    counts = jnp.minimum(counts, available)
    slots = jnp.arange(REACH, dtype=jnp.int32)[None, :]
    owner = jnp.where(slots < counts[:, None], reader + picked, -1)
    return owner.astype(jnp.int32)


def set_ends(result, key, smallest, top_value):
    shape = result.shape
    index_at = [jax.random.randint(jax.random.fold_in(key, axis), (), 0, shape[axis]) for axis in range(len(shape))]
    result = result.at[tuple(index_at)].set(smallest)
    longest = shape.index(max(shape))
    index_at[longest] = (index_at[longest] + 1) % shape[longest]
    return result.at[tuple(index_at)].set(top_value)


def levels(key, dims, shards, smallest, high):
    gain = 1.0
    for axis_at, parts in shards:
        steps = jax.random.uniform(jax.random.fold_in(jax.random.fold_in(key, 6), axis_at), (parts,), jnp.float32, smallest / len(shards), high / len(shards))
        gain = gain * jnp.repeat(jnp.exp(steps), dims[axis_at] // parts).reshape((-1,) + (1,) * (len(dims) - 1 - axis_at))
    return gain


def scatter_about(key, dims, width, most, cuts=(), held_as=jnp.bfloat16):
    drawn = width * jax.random.normal(key, dims, jnp.float32)
    if cuts:
        drawn = drawn * levels(key, dims, cuts, -0.22, 0.18)
    return jnp.clip(drawn, -most, most).astype(held_as)


def setup_inputs(seed: int = 0) -> dict:
    seeds = jax.random.split(jax.random.key(seed), 4)
    return {
        "traces": scatter_about(seeds[0], (BLOCKS, WINDOWS, BLOCK, WIN), 1.0, 6.0, ((0, 16), (1, 2))),
        "valid_mask": set_ends((jax.random.randint(seeds[1], (BLOCKS, WINDOWS, WIN), 0, 8) < 7).astype(jnp.int32), jax.random.fold_in(seeds[1], 1), 0, 1),
        "pair_owner": draw_pair_owner(jax.random.fold_in(seeds[3], 71), 0),
    }


water_level = 0.05
eps = 1e-06

def forward_table():
    samples = jnp.arange(WIN, dtype=jnp.int32)
    bins = jnp.arange(1, NF + 1, dtype=jnp.int32)
    phase = samples[:, None] * bins[None, :] % WIN
    angle = phase.astype(jnp.float32) * jnp.float32(2.0 * math.pi / WIN)
    return jnp.concatenate([jnp.cos(angle), -jnp.sin(angle)], axis=1).astype(jnp.bfloat16)

def inverse_table():
    bins = jnp.arange(1, NF + 1, dtype=jnp.int32)
    offsets = jnp.arange(LAGS, dtype=jnp.int32) - MAXLAG
    phase = bins[:, None] * offsets[None, :] % WIN
    angle = phase.astype(jnp.float32) * jnp.float32(2.0 * math.pi / WIN)
    factor = jnp.float32(1.0 / math.sqrt(WINDOWS * NF))
    return jnp.concatenate([jnp.cos(angle), -jnp.sin(angle)], axis=0) * factor

def whiten(block_traces, block_mask, forward):
    masked = block_traces * block_mask[:, None, :].astype(jnp.bfloat16)
    wins, chans, samples = masked.shape
    spectra = jnp.dot(masked.reshape(wins * chans, samples), forward, preferred_element_type=jnp.float32)
    spectra = spectra.reshape(wins, chans, 2 * NF)
    real_part = spectra[..., :NF]
    imag_part = spectra[..., NF:]
    amplitude = jnp.sqrt(real_part * real_part + imag_part * imag_part)
    padded = jnp.pad(amplitude, ((0, 0), (0, 0), (SMOOTH, SMOOTH)))
    smooth = padded[..., 0:NF]
    for j in range(1, 2 * SMOOTH + 1):
        smooth = smooth + padded[..., j:j + NF]
    smooth = smooth / jnp.float32(2 * SMOOTH + 1)
    divisor = smooth + water_level * lax.optimization_barrier(jnp.mean(amplitude, axis=-1, keepdims=True)) + eps
    return (spectra / jnp.concatenate([divisor, divisor], axis=-1)).astype(jnp.bfloat16)

def cross_spectrum(own_spec, other_spec):
    left = own_spec.astype(jnp.float32)
    right = other_spec.astype(jnp.float32)
    swapped = jnp.concatenate([right[..., NF:], right[..., :NF]], axis=-1)
    direct = jnp.einsum('wcf,wcf->cf', left, right)
    crossed = jnp.einsum('wcf,wcf->cf', left, swapped)
    return jnp.concatenate([direct[:, :NF] + direct[:, NF:], crossed[:, :NF] - crossed[:, NF:]], axis=-1)

def reference(traces, valid_mask, pair_owner):
    forward = forward_table()
    inverse = inverse_table()
    white_all = lax.map(lambda item: whiten(item[0], item[1], forward), (traces, valid_mask))

    def one_reader(reader):
        own_spec = white_all[reader]
        owners = pair_owner[reader]
        stacks = []
        for slot in range(REACH):
            owner = owners[slot]
            other = white_all[jnp.maximum(owner, 0)]
            keep = (owner >= 0).astype(jnp.float32)
            stacks.append(cross_spectrum(own_spec, other) * keep)
        cross = jnp.stack(stacks, axis=0)
        return jnp.einsum('pck,kl->plc', cross, inverse, precision=lax.Precision.HIGHEST)
    return lax.map(one_reader, jnp.arange(BLOCKS, dtype=jnp.int32))
```

```python
import functools
import math

import jax
import jax.numpy as jnp
import ml_dtypes
import numpy as np
from jax import lax
from jax.experimental import pallas as pl
from jax.experimental.pallas import tpu as pltpu
from jax.sharding import PartitionSpec as P

NF = 256
MAXLAG = 50
LAGS = 2 * MAXLAG + 1
SMOOTH = 4
REACH = 4
LAG_PAD = 128
LAG_ROWS = 104

WATER = 0.05
EPS = 1e-06

MESH = pl.DeviceIdType.MESH

BIG = [
    (0, 1), (0, 2), (0, 3), (0, 4),
    (1, 2), (1, 3), (1, 4), (1, 5),
    (2, 3), (2, 4), (2, 5),
    (3, 4), (3, 5),
    (4, 5),
]
SMALL = [(0, 2), (1, 2), (1, 3)]


def forward_table(samples_count):
    samples = np.arange(samples_count)
    bins = np.arange(1, NF + 1)
    angle = (samples[:, None] * bins[None, :] % samples_count) * (2.0 * math.pi / samples_count)
    return np.concatenate([np.cos(angle), -np.sin(angle)], axis=1).astype(ml_dtypes.bfloat16)


def inverse_table(samples_count, windows_all):
    bins = np.arange(1, NF + 1)
    offsets = np.arange(LAGS) - MAXLAG
    angle = (bins[:, None] * offsets[None, :] % samples_count) * (2.0 * math.pi / samples_count)
    table = np.concatenate([np.cos(angle), -np.sin(angle)], axis=0) / math.sqrt(windows_all * NF)
    return np.pad(table, ((0, 0), (0, LAG_PAD - LAGS))).astype(np.float32)


def smooth_table():
    bins = np.arange(NF)
    band = (np.abs(bins[:, None] - bins[None, :]) <= SMOOTH).astype(np.float32)
    return np.concatenate([band, np.ones((NF, NF), np.float32)], axis=0).astype(ml_dtypes.bfloat16)


def kernel(
    groups, planes,
    traces, mask, forward, smoother, inverse,
    out,
    tbuf, fbuf, maskx, own, big, small, cross_big, cross_small, res_big, res_small, rbuf,
    tsem, fsem, send_sem, big_sem, small_sem, rsend, rsem,
):
    wins = traces.shape[0]
    rows = own.shape[3]
    me = lax.axis_index("chan")
    tm = lax.axis_index("tm")
    core = lax.rem(me, 2)
    y = lax.rem(me // 2, 2)
    z = me // 4
    depth = groups // 4
    has_up = z < depth - 1
    has_down = z > 0
    has_big = jnp.where(y == 0, depth - 1 - z, z) > 0
    has_small = jnp.where(y == 0, z, depth - 1 - z) > 0
    big_base = 4 * z - 2 * y
    small_base = 4 * z - 4 + 6 * y

    def channel_start(p):
        return (p % 2) * 64 + ((p // 2) % 2) * 32 + (p // 4) * 16

    def load(p):
        return pltpu.make_async_copy(
            traces.at[:, pl.ds(pl.multiple_of(channel_start(p), 16), 16), :], tbuf.at[p], tsem.at[p]
        )

    load(0).start()
    table_copy = pltpu.make_async_copy(forward, fbuf, fsem)
    table_copy.start()
    for p in range(1, 8):
        load(p).start()

    barrier = pltpu.get_barrier_semaphore()
    for dz in (-1, 0, 1):
        zz = z + dz

        @pl.when((zz >= 0) & (zz < depth))
        def _():
            for k in range(4):
                for t in range(planes):

                    @pl.when((zz * 4 + k != me) | (t != tm))
                    def _():
                        pl.semaphore_signal(
                            barrier, inc=1, device_id={"chan": zz * 4 + k, "tm": t}, device_id_type=MESH
                        )

    near = 1 + has_up.astype(jnp.int32) + has_down.astype(jnp.int32)
    partners = near * (4 * planes) - 1

    for w in range(wins):
        row = mask[w : w + 1, :].astype(jnp.float32)
        maskx[w] = jnp.broadcast_to(row, (16, row.shape[1])).astype(jnp.bfloat16)

    def chunk_copies(e, c, j, act, act_local):
        src = own.at[e, c, j]
        slot = (e * 2 + c) * 4 + j
        is_big = e == y
        zt = z + 2 * e - 1
        has_z = (zt >= 0) & (zt < depth)

        def remote(dst, kind, recv, chan):
            act(
                pltpu.make_async_remote_copy(
                    src_ref=src, dst_ref=dst, send_sem=send_sem.at[slot, kind], recv_sem=recv,
                    device_id={"chan": chan}, device_id_type=MESH,
                )
            )

        @pl.when(is_big & has_z)
        def _():
            remote(big.at[j, 4 * (1 - y) + core], 0, big_sem.at[j], zt * 4 + y * 2 + c)

        @pl.when(jnp.logical_not(is_big))
        def _():
            remote(big.at[j, 2 + core], 1, big_sem.at[j], z * 4 + (1 - y) * 2 + c)

        @pl.when(jnp.logical_not(is_big) & has_z)
        def _():
            remote(small.at[j, 2 * (1 - e) + core], 0, small_sem.at[j], zt * 4 + y * 2 + c)

        @pl.when(is_big & (c != core))
        def _():
            remote(big.at[j, 4 * y + core], 2, big_sem.at[j], z * 4 + y * 2 + c)

        @pl.when(jnp.logical_not(is_big) & has_small & (c != core))
        def _():
            remote(small.at[j, 2 * (1 - y) + core], 2, small_sem.at[j], z * 4 + y * 2 + c)

        if act_local:

            @pl.when(is_big & (c == core))
            def _():
                pltpu.make_async_copy(src, big.at[j, 4 * y + core], big_sem.at[j]).start()

            @pl.when(jnp.logical_not(is_big) & has_small & (c == core))
            def _():
                pltpu.make_async_copy(src, small.at[j, 2 * (1 - y) + core], small_sem.at[j]).start()

    def start(copy):
        copy.start()

    def wait_send(copy):
        copy.wait_send()

    table_copy.wait()

    def produce(p, carry):
        e = lax.rem(p, 2)
        c = lax.rem(p // 2, 2)
        half = p // 4
        load(p).wait()
        x = (tbuf[p] * maskx[...]).reshape(wins * 16, tbuf.shape[3])
        spectra = jnp.dot(x, fbuf[...], preferred_element_type=jnp.float32)
        real = spectra[:, :NF]
        imag = spectra[:, NF:]
        amplitude = jnp.sqrt(real * real + imag * imag)
        scaled = amplitude * jnp.float32((2 * SMOOTH + 1) * WATER / NF)
        both = jnp.concatenate([amplitude.astype(jnp.bfloat16), scaled.astype(jnp.bfloat16)], axis=1)
        total = jnp.dot(both, smoother[...], preferred_element_type=jnp.float32)
        gain = jnp.float32(2 * SMOOTH + 1) / (total + jnp.float32((2 * SMOOTH + 1) * EPS))
        for part, lo in ((real, 0), (imag, NF)):
            white = (part * gain).reshape(wins, 16, NF)
            for h in range(2):
                own[e, c, 2 * half + h, :, lo : lo + NF] = (
                    white[:, 8 * h : 8 * h + 8, :].reshape(wins * 8, NF).astype(jnp.bfloat16)
                )

        @pl.when(p == 0)
        def _():
            pl.semaphore_wait(barrier, partners)

        chunk_copies(e, c, half, start, True)
        return carry

    lax.fori_loop(0, 8, produce, 0)

    def cross(buf, j, pairs, result):
        used = sorted({s for pair in pairs for s in pair})
        for f in range(NF // 128):
            lo = f * 128

            def step(i, sums):
                r = pl.ds(pl.multiple_of(i * 16, 16), 16)
                re = {s: buf[j, s, r, lo : lo + 128].astype(jnp.float32) for s in used}
                im = {s: buf[j, s, r, NF + lo : NF + lo + 128].astype(jnp.float32) for s in used}
                new = []
                for n, (a, b) in enumerate(pairs):
                    direct = re[a] * re[b] + im[a] * im[b]
                    crossed = re[a] * im[b] - im[a] * re[b]
                    new.append(sums[2 * n] + (direct[:8] + direct[8:]))
                    new.append(sums[2 * n + 1] + (crossed[:8] + crossed[8:]))
                return tuple(new)

            zero = jnp.zeros((8, 128), jnp.float32)
            sums = lax.fori_loop(0, rows // 16, step, (zero,) * (2 * len(pairs)))
            for n in range(len(pairs)):
                result[8 * n : 8 * n + 8, lo : lo + 128] = sums[2 * n]
                result[8 * n : 8 * n + 8, NF + lo : NF + lo + 128] = sums[2 * n + 1]

    def lags(result):
        return jnp.dot(
            result[...], inverse[...], precision=lax.Precision.HIGHEST, preferred_element_type=jnp.float32
        ).reshape(-1, 8, LAG_PAD)

    def messages(res, j, base, e, first, listed, act, act_local):
        at = pl.ds(pl.multiple_of(e * 64 + core * 32 + j * 8, 8), 8)
        for k, (s, pair, count, distance) in enumerate(listed):
            chan = base + s
            src = res.at[j, pl.ds(pair, count)]
            dst = rbuf.at[tm, pl.ds(distance, count), at]
            for t in range(planes):
                mine = (chan == me) & (t == tm)

                @pl.when(jnp.logical_not(mine))
                def _():
                    act(
                        pltpu.make_async_remote_copy(
                            src_ref=src, dst_ref=dst, send_sem=rsend.at[first + k, t], recv_sem=rsem,
                            device_id={"chan": chan, "tm": t}, device_id_type=MESH,
                        )
                    )

                if act_local:

                    @pl.when(mine)
                    def _():
                        pltpu.make_async_copy(src, dst, rsem).start()

    def big_messages(j, act, act_local):
        send = functools.partial(messages, res_big, j, big_base, y, 0)

        @pl.when((y == 0) & has_big)
        def _():
            send([(0, 0, 4, 0), (1, 4, 4, 0), (2, 8, 3, 0), (3, 11, 2, 0)], act, act_local)

        @pl.when((y == 0) & jnp.logical_not(has_big))
        def _():
            send([(0, 0, 3, 0), (1, 4, 2, 0), (2, 8, 1, 0)], act, act_local)

        @pl.when((y == 1) & has_big)
        def _():
            send([(0, 1, 3, 1), (1, 4, 4, 0), (2, 8, 3, 0), (3, 11, 2, 0), (4, 13, 1, 0)], act, act_local)

        @pl.when((y == 1) & jnp.logical_not(has_big))
        def _():
            send([(2, 8, 3, 0), (3, 11, 2, 0), (4, 13, 1, 0)], act, act_local)

    def small_messages(j, act, act_local):
        @pl.when(has_small)
        def _():
            messages(res_small, j, small_base, 1 - y, 5, [(0, 0, 1, 3), (1, 1, 2, 2)], act, act_local)

    def correlate(j, carry):
        @pl.when(has_small)
        def _():
            pltpu.make_async_copy(small.at[j], small.at[j], small_sem.at[j]).wait()

        @pl.when(has_big)
        def _():
            pltpu.make_async_copy(big.at[j], big.at[j], big_sem.at[j]).wait()

        @pl.when(jnp.logical_not(has_big))
        def _():
            there = big.at[j, pl.ds(2 * y, 4)]
            pltpu.make_async_copy(there, there, big_sem.at[j]).wait()

        @pl.when(j < 2)
        def _():
            for c in range(2):
                for e in range(2):
                    chunk_copies(e, c, j + 2, start, True)

        @pl.when(j > 0)
        def _():
            big_messages(j - 1, wait_send, False)
            small_messages(j - 1, wait_send, False)

        cross(big, j, BIG, cross_big)
        res_big[j] = lags(cross_big)
        big_messages(j, start, True)

        @pl.when(has_small)
        def _():
            cross(small, j, SMALL, cross_small)
            res_small[j] = lags(cross_small)

        small_messages(j, start, True)
        return carry

    lax.fori_loop(0, 4, correlate, 0)
    big_messages(3, wait_send, False)
    small_messages(3, wait_send, False)

    def drain(n, carry):
        chunk_copies(n // 8, lax.rem(n // 4, 2), lax.rem(n, 4), wait_send, False)
        return carry

    lax.fori_loop(0, 16, drain, 0)

    valid = jnp.minimum(REACH, groups - 1 - me)
    for n in range(1, REACH + 1):

        @pl.when(valid == n)
        def _():
            whole = rbuf.at[:, pl.ds(0, n)]
            pltpu.make_async_copy(whole, whole, rsem).wait()

    for d in range(REACH):

        @pl.when(d < valid)
        def _():
            total = rbuf[0, d]
            for t in range(1, planes):
                total = total + rbuf[t, d]
            out[d] = total.T[:LAG_ROWS]

        @pl.when(d >= valid)
        def _():
            out[d] = jnp.zeros(out.shape[1:], jnp.float32)


def body(traces, valid_mask, pair_owner):
    _, wins, chans, samples = traces.shape
    groups = lax.axis_size("chan")
    planes = lax.axis_size("tm")
    rows = wins * 8
    vmem = pl.BlockSpec(memory_space=pltpu.VMEM)
    hbm = pl.BlockSpec(memory_space=pl.ANY)
    f32, bf16 = jnp.float32, jnp.bfloat16
    sums = pl.pallas_call(
        functools.partial(kernel, groups, planes),
        out_shape=jax.ShapeDtypeStruct((REACH, LAG_ROWS, chans), f32),
        in_specs=[hbm, vmem, hbm, vmem, vmem],
        out_specs=vmem,
        scratch_shapes=[
            pltpu.VMEM((8, wins, 16, samples), bf16),
            pltpu.VMEM((samples, 2 * NF), bf16),
            pltpu.VMEM((wins, 16, samples), bf16),
            pltpu.VMEM((2, 2, 4, rows, 2 * NF), bf16),
            pltpu.VMEM((4, 6, rows, 2 * NF), bf16),
            pltpu.VMEM((4, 4, rows, 2 * NF), bf16),
            pltpu.VMEM((len(BIG) * 8, 2 * NF), f32),
            pltpu.VMEM((len(SMALL) * 8, 2 * NF), f32),
            pltpu.VMEM((4, len(BIG), 8, LAG_PAD), f32),
            pltpu.VMEM((4, len(SMALL), 8, LAG_PAD), f32),
            pltpu.VMEM((planes, REACH, chans, LAG_PAD), f32),
            pltpu.SemaphoreType.DMA((8,)),
            pltpu.SemaphoreType.DMA,
            pltpu.SemaphoreType.DMA((16, 3)),
            pltpu.SemaphoreType.DMA((4,)),
            pltpu.SemaphoreType.DMA((4,)),
            pltpu.SemaphoreType.DMA((7, planes)),
            pltpu.SemaphoreType.DMA,
        ],
        compiler_params=pltpu.CompilerParams(
            collective_id=0, has_side_effects=True, vmem_limit_bytes=56 * 1024 * 1024
        ),
        name="correlate",
    )(
        traces[0],
        valid_mask[0],
        jnp.asarray(forward_table(samples)),
        jnp.asarray(smooth_table()),
        jnp.asarray(inverse_table(samples, wins * planes)),
    )
    reader = lax.axis_index("chan")
    owners = pair_owner[0]
    result = jnp.zeros((REACH, LAGS, chans), f32)
    for d in range(REACH):
        chosen = (owners == reader + d + 1)[:, None, None]
        result = result + jnp.where(chosen, sums[d, :LAGS][None], jnp.float32(0))
    return result[None]


def solution(mesh):
    return jax.shard_map(
        body,
        mesh=mesh,
        in_specs=(P("chan", "tm", None, None), P("chan", "tm", None), P("chan", None)),
        out_specs=P("chan", None, None, None),
        check_vma=False,
    )
```

```python
import functools
import math

import jax
import jax.numpy as jnp
import ml_dtypes
import numpy as np
from jax import lax
from jax.experimental import pallas as pl
from jax.experimental.pallas import tpu as pltpu
from jax.sharding import PartitionSpec as P

NF = 256
MAXLAG = 50
LAGS = 2 * MAXLAG + 1
SMOOTH = 4
REACH = 4
LAG_PAD = 128

WATER = 0.05
EPS = 1e-06

MESH = pl.DeviceIdType.MESH

BIG = [
    (0, 1), (0, 2), (0, 3), (0, 4),
    (1, 2), (1, 3), (1, 4), (1, 5),
    (2, 3), (2, 4), (2, 5),
    (3, 4), (3, 5),
    (4, 5),
]
SMALL = [(0, 2), (1, 2), (1, 3)]


def forward_table(samples_count):
    samples = np.arange(samples_count)
    bins = np.arange(1, NF + 1)
    angle = (samples[:, None] * bins[None, :] % samples_count) * (2.0 * math.pi / samples_count)
    return np.concatenate([np.cos(angle), -np.sin(angle)], axis=1).astype(ml_dtypes.bfloat16)


def inverse_table(samples_count, windows_all):
    bins = np.arange(1, NF + 1)
    offsets = np.arange(LAGS) - MAXLAG
    angle = (bins[:, None] * offsets[None, :] % samples_count) * (2.0 * math.pi / samples_count)
    table = np.concatenate([np.cos(angle), -np.sin(angle)], axis=0) / math.sqrt(windows_all * NF)
    table = np.pad(table, ((0, 0), (0, LAG_PAD - LAGS))).astype(np.float32)
    high = table.astype(ml_dtypes.bfloat16)
    low = (table - high.astype(np.float32)).astype(ml_dtypes.bfloat16)
    return np.concatenate([high, high, low], axis=0)


def smooth_table():
    bins = np.arange(NF)
    band = (np.abs(bins[:, None] - bins[None, :]) <= SMOOTH).astype(np.float32)
    return np.concatenate([band, np.ones((NF, NF), np.float32)], axis=0).astype(ml_dtypes.bfloat16)


def kernel(
    groups, planes,
    traces, mask, forward, smoother, inverse,
    out,
    tbuf, fbuf, maskx, own, big, small, cross_sum, res, rbuf,
    tsem, fsem, send_sem, big_sem, small_sem, rsend, rsem,
):
    wins = traces.shape[0]
    rows = own.shape[3]
    me = lax.axis_index("chan")
    tm = lax.axis_index("tm")
    core = lax.rem(me, 2)
    y = lax.rem(me // 2, 2)
    z = me // 4
    depth = groups // 4
    has_up = z < depth - 1
    has_down = z > 0
    has_big = jnp.where(y == 0, depth - 1 - z, z) > 0
    has_small = jnp.where(y == 0, z, depth - 1 - z) > 0
    big_base = 4 * z - 2 * y
    small_base = 4 * z - 4 + 6 * y

    def channel_start(p):
        return (p % 2) * 64 + ((p // 2) % 2) * 32 + (p // 4) * 16

    def load(p):
        return pltpu.make_async_copy(
            traces.at[:, pl.ds(pl.multiple_of(channel_start(p), 16), 16), :], tbuf.at[p], tsem.at[p]
        )

    load(0).start()
    table_copy = pltpu.make_async_copy(forward, fbuf, fsem)
    table_copy.start()
    for p in range(1, 8):
        load(p).start()

    barrier = pltpu.get_barrier_semaphore()
    for dz in (-1, 0, 1):
        zz = z + dz

        @pl.when((zz >= 0) & (zz < depth))
        def _():
            for k in range(4):
                for t in range(planes):

                    @pl.when((zz * 4 + k != me) | (t != tm))
                    def _():
                        pl.semaphore_signal(
                            barrier, inc=1, device_id={"chan": zz * 4 + k, "tm": t}, device_id_type=MESH
                        )

    near = 1 + has_up.astype(jnp.int32) + has_down.astype(jnp.int32)
    partners = near * (4 * planes) - 1

    for w in range(wins):
        row = mask[w : w + 1, :].astype(jnp.float32)
        maskx[w] = jnp.broadcast_to(row, (16, row.shape[1])).astype(jnp.bfloat16)

    def chunk_copies(e, c, j, act, act_local):
        src = own.at[e, c, j]
        slot = (e * 2 + c) * 4 + j
        is_big = e == y
        zt = z + 2 * e - 1
        has_z = (zt >= 0) & (zt < depth)

        def remote(dst, kind, recv, chan):
            act(
                pltpu.make_async_remote_copy(
                    src_ref=src, dst_ref=dst, send_sem=send_sem.at[slot, kind], recv_sem=recv,
                    device_id={"chan": chan}, device_id_type=MESH,
                )
            )

        @pl.when(is_big & has_z)
        def _():
            remote(big.at[j, 4 * (1 - y) + core], 0, big_sem.at[j], zt * 4 + y * 2 + c)

        @pl.when(jnp.logical_not(is_big))
        def _():
            remote(big.at[j, 2 + core], 1, big_sem.at[j], z * 4 + (1 - y) * 2 + c)

        @pl.when(jnp.logical_not(is_big) & has_z)
        def _():
            remote(small.at[j, 2 * (1 - e) + core], 0, small_sem.at[j], zt * 4 + y * 2 + c)

        @pl.when(is_big & (c != core))
        def _():
            remote(big.at[j, 4 * y + core], 2, big_sem.at[j], z * 4 + y * 2 + c)

        @pl.when(jnp.logical_not(is_big) & has_small & (c != core))
        def _():
            remote(small.at[j, 2 * (1 - y) + core], 2, small_sem.at[j], z * 4 + y * 2 + c)

        if act_local:

            @pl.when(is_big & (c == core))
            def _():
                pltpu.make_async_copy(src, big.at[j, 4 * y + core], big_sem.at[j]).start()

            @pl.when(jnp.logical_not(is_big) & has_small & (c == core))
            def _():
                pltpu.make_async_copy(src, small.at[j, 2 * (1 - y) + core], small_sem.at[j]).start()

    def start(copy):
        copy.start()

    def wait_send(copy):
        copy.wait_send()

    table_copy.wait()

    def produce(p, carry):
        e = lax.rem(p, 2)
        c = lax.rem(p // 2, 2)
        half = p // 4
        load(p).wait()
        x = (tbuf[p] * maskx[...]).reshape(wins * 16, tbuf.shape[3])
        spectra = jnp.dot(x, fbuf[...], preferred_element_type=jnp.float32)
        real = spectra[:, :NF]
        imag = spectra[:, NF:]
        amplitude = jnp.sqrt(real * real + imag * imag)
        scaled = amplitude * jnp.float32((2 * SMOOTH + 1) * WATER / NF)
        both = jnp.concatenate([amplitude.astype(jnp.bfloat16), scaled.astype(jnp.bfloat16)], axis=1)
        total = jnp.dot(both, smoother[...], preferred_element_type=jnp.float32)
        gain = jnp.float32(2 * SMOOTH + 1) / (total + jnp.float32((2 * SMOOTH + 1) * EPS))
        for part, lo in ((real, 0), (imag, NF)):
            white = (part * gain).reshape(wins, 16, NF)
            for h in range(2):
                own[e, c, 2 * half + h, :, lo : lo + NF] = (
                    white[:, 8 * h : 8 * h + 8, :].reshape(wins * 8, NF).astype(jnp.bfloat16)
                )

        @pl.when(p == 0)
        def _():
            pl.semaphore_wait(barrier, partners)

        chunk_copies(e, c, half, start, True)
        return carry

    lax.fori_loop(0, 8, produce, 0)

    def send_rest(n, carry):
        chunk_copies(lax.rem(n, 2), lax.rem(n // 2, 2), 2 + n // 4, start, True)
        return carry

    lax.fori_loop(0, 8, send_rest, 0)

    def cross(buf, j, pairs, first):
        used = sorted({s for pair in pairs for s in pair})
        for f in range(NF // 128):
            lo = f * 128

            def step(i, sums):
                r = pl.ds(pl.multiple_of(i * 16, 16), 16)
                re = {s: buf[j, s, r, lo : lo + 128].astype(jnp.float32) for s in used}
                im = {s: buf[j, s, r, NF + lo : NF + lo + 128].astype(jnp.float32) for s in used}
                new = []
                for n, (a, b) in enumerate(pairs):
                    direct = re[a] * re[b] + im[a] * im[b]
                    crossed = re[a] * im[b] - im[a] * re[b]
                    new.append(sums[2 * n] + (direct[:8] + direct[8:]))
                    new.append(sums[2 * n + 1] + (crossed[:8] + crossed[8:]))
                return tuple(new)

            zero = jnp.zeros((8, 128), jnp.float32)
            sums = lax.fori_loop(0, rows // 16, step, (zero,) * (2 * len(pairs)))
            for n in range(len(pairs)):
                cross_sum[first + 8 * n : first + 8 * n + 8, lo : lo + 128] = sums[2 * n]
                cross_sum[first + 8 * n : first + 8 * n + 8, NF + lo : NF + lo + 128] = sums[2 * n + 1]

    def lags():
        value = cross_sum[...]
        high = value.astype(jnp.bfloat16)
        low = (value - high.astype(jnp.float32)).astype(jnp.bfloat16)
        return jnp.dot(
            jnp.concatenate([high, low, high], axis=1), inverse[...], preferred_element_type=jnp.float32
        ).reshape(-1, 8, LAG_PAD)

    def messages(j, base, e, first, listed, act, act_local):
        at = pl.ds(pl.multiple_of(e * 64 + core * 32 + j * 8, 8), 8)
        for k, (s, pair, count, distance) in enumerate(listed):
            chan = base + s
            src = res.at[j, pl.ds(pair, count)]
            dst = rbuf.at[tm, pl.ds(distance, count), at]
            for t in range(planes):
                mine = (chan == me) & (t == tm)

                @pl.when(jnp.logical_not(mine))
                def _():
                    act(
                        pltpu.make_async_remote_copy(
                            src_ref=src, dst_ref=dst, send_sem=rsend.at[first + k, t], recv_sem=rsem,
                            device_id={"chan": chan, "tm": t}, device_id_type=MESH,
                        )
                    )

                if act_local:

                    @pl.when(mine)
                    def _():
                        pltpu.make_async_copy(src, dst, rsem).start()

    def big_messages(j, act, act_local):
        send = functools.partial(messages, j, big_base, y, 0)

        @pl.when((y == 0) & has_big)
        def _():
            send([(0, 0, 4, 0), (1, 4, 4, 0), (2, 8, 3, 0), (3, 11, 2, 0)], act, act_local)

        @pl.when((y == 0) & jnp.logical_not(has_big))
        def _():
            send([(0, 0, 3, 0), (1, 4, 2, 0), (2, 8, 1, 0)], act, act_local)

        @pl.when((y == 1) & has_big)
        def _():
            send([(0, 1, 3, 1), (1, 4, 4, 0), (2, 8, 3, 0), (3, 11, 2, 0), (4, 13, 1, 0)], act, act_local)

        @pl.when((y == 1) & jnp.logical_not(has_big))
        def _():
            send([(2, 8, 3, 0), (3, 11, 2, 0), (4, 13, 1, 0)], act, act_local)

    def small_messages(j, act, act_local):
        @pl.when(has_small)
        def _():
            messages(j, small_base, 1 - y, 5, [(0, 14, 1, 3), (1, 15, 2, 2)], act, act_local)

    def correlate(j, carry):
        @pl.when(has_small)
        def _():
            pltpu.make_async_copy(small.at[j], small.at[j], small_sem.at[j]).wait()

        @pl.when(has_big)
        def _():
            pltpu.make_async_copy(big.at[j], big.at[j], big_sem.at[j]).wait()

        @pl.when(jnp.logical_not(has_big))
        def _():
            there = big.at[j, pl.ds(2 * y, 4)]
            pltpu.make_async_copy(there, there, big_sem.at[j]).wait()

        @pl.when(j > 0)
        def _():
            big_messages(j - 1, wait_send, False)
            small_messages(j - 1, wait_send, False)

        cross(big, j, BIG, 0)

        @pl.when(has_small)
        def _():
            cross(small, j, SMALL, 8 * len(BIG))

        res[j] = lags()
        big_messages(j, start, True)
        small_messages(j, start, True)
        return carry

    lax.fori_loop(0, 4, correlate, 0)
    big_messages(3, wait_send, False)
    small_messages(3, wait_send, False)

    def drain(n, carry):
        chunk_copies(n // 8, lax.rem(n // 4, 2), lax.rem(n, 4), wait_send, False)
        return carry

    lax.fori_loop(0, 16, drain, 0)

    valid = jnp.minimum(REACH, groups - 1 - me)
    for n in range(1, REACH + 1):

        @pl.when(valid == n)
        def _():
            whole = rbuf.at[:, pl.ds(0, n)]
            pltpu.make_async_copy(whole, whole, rsem).wait()

    for d in range(REACH):

        @pl.when(d < valid)
        def _():
            total = rbuf[0, d]
            for t in range(1, planes):
                total = total + rbuf[t, d]
            out[d] = total.T[:LAGS]

        @pl.when(d >= valid)
        def _():
            out[d] = jnp.zeros(out.shape[1:], jnp.float32)


def body(traces, valid_mask, pair_owner):
    _, wins, chans, samples = traces.shape
    groups = lax.axis_size("chan")
    planes = lax.axis_size("tm")
    rows = wins * 8
    vmem = pl.BlockSpec(memory_space=pltpu.VMEM)
    hbm = pl.BlockSpec(memory_space=pl.ANY)
    f32, bf16 = jnp.float32, jnp.bfloat16
    sums = pl.pallas_call(
        functools.partial(kernel, groups, planes),
        out_shape=jax.ShapeDtypeStruct((REACH, LAGS, chans), f32),
        in_specs=[hbm, vmem, hbm, vmem, vmem],
        out_specs=vmem,
        scratch_shapes=[
            pltpu.VMEM((8, wins, 16, samples), bf16),
            pltpu.VMEM((samples, 2 * NF), bf16),
            pltpu.VMEM((wins, 16, samples), bf16),
            pltpu.VMEM((2, 2, 4, rows, 2 * NF), bf16),
            pltpu.VMEM((4, 6, rows, 2 * NF), bf16),
            pltpu.VMEM((4, 4, rows, 2 * NF), bf16),
            pltpu.VMEM(((len(BIG) + len(SMALL)) * 8, 2 * NF), f32),
            pltpu.VMEM((4, len(BIG) + len(SMALL), 8, LAG_PAD), f32),
            pltpu.VMEM((planes, REACH, chans, LAG_PAD), f32),
            pltpu.SemaphoreType.DMA((8,)),
            pltpu.SemaphoreType.DMA,
            pltpu.SemaphoreType.DMA((16, 3)),
            pltpu.SemaphoreType.DMA((4,)),
            pltpu.SemaphoreType.DMA((4,)),
            pltpu.SemaphoreType.DMA((7, planes)),
            pltpu.SemaphoreType.DMA,
        ],
        compiler_params=pltpu.CompilerParams(
            collective_id=0, has_side_effects=True, vmem_limit_bytes=56 * 1024 * 1024
        ),
        name="correlate",
    )(
        traces[0],
        valid_mask[0],
        jnp.asarray(forward_table(samples)),
        jnp.asarray(smooth_table()),
        jnp.asarray(inverse_table(samples, wins * planes)),
    )
    reader = lax.axis_index("chan")
    owners = pair_owner[0]
    result = jnp.zeros((REACH, LAGS, chans), f32)
    for d in range(REACH):
        chosen = (owners == reader + d + 1)[:, None, None]
        result = result + jnp.where(chosen, sums[d][None], jnp.float32(0))
    return result[None]


def solution(mesh):
    return jax.shard_map(
        body,
        mesh=mesh,
        in_specs=(P("chan", "tm", None, None), P("chan", "tm", None), P("chan", None)),
        out_specs=P("chan", None, None, None),
        check_vma=False,
    )
```

```python
import functools
import math

import jax
import jax.numpy as jnp
import ml_dtypes
import numpy as np
from jax import lax
from jax.experimental import pallas as pl
from jax.experimental.pallas import tpu as pltpu
from jax.sharding import PartitionSpec as P

NF = 256
MAXLAG = 50
LAGS = 2 * MAXLAG + 1
SMOOTH = 4
REACH = 4
LAG_PAD = 128
AHEAD = 4

WATER = 0.05
EPS = 1e-06

MESH = pl.DeviceIdType.MESH

BIG = [
    (0, 1), (0, 2), (0, 3), (0, 4),
    (1, 2), (1, 3), (1, 4), (1, 5),
    (2, 3), (2, 4), (2, 5),
    (3, 4), (3, 5),
    (4, 5),
]
SMALL = [(0, 2), (1, 2), (1, 3)]


def forward_table(samples_count):
    samples = np.arange(samples_count)
    bins = np.arange(1, NF + 1)
    angle = (samples[:, None] * bins[None, :] % samples_count) * (2.0 * math.pi / samples_count)
    return np.concatenate([np.cos(angle), -np.sin(angle)], axis=1).astype(ml_dtypes.bfloat16)


def inverse_table(samples_count, windows_all):
    bins = np.arange(1, NF + 1)
    offsets = np.arange(LAGS) - MAXLAG
    angle = (bins[:, None] * offsets[None, :] % samples_count) * (2.0 * math.pi / samples_count)
    table = np.concatenate([np.cos(angle), -np.sin(angle)], axis=0) / math.sqrt(windows_all * NF)
    table = np.pad(table, ((0, 0), (0, LAG_PAD - LAGS))).astype(np.float32)
    high = table.astype(ml_dtypes.bfloat16)
    low = (table - high.astype(np.float32)).astype(ml_dtypes.bfloat16)
    tiles = NF // 128
    parts = []
    for f in range(tiles):
        picked = np.concatenate([np.arange(f * 128, f * 128 + 128), np.arange(NF + f * 128, NF + f * 128 + 128)])
        parts.append(np.concatenate([high[picked], high[picked], low[picked]], axis=0))
    return np.stack(parts)


def smooth_table():
    bins = np.arange(NF)
    band = (np.abs(bins[:, None] - bins[None, :]) <= SMOOTH).astype(np.float32)
    return np.concatenate([band, np.ones((NF, NF), np.float32)], axis=0).astype(ml_dtypes.bfloat16)


def kernel(
    groups, planes,
    traces, mask, owners, forward, smoother_hbm, inverse_hbm,
    out,
    tbuf, fbuf, smoother, inverse, maskx, own, big, small, cross_sum, res, rbuf,
    tsem, fsem, send_sem, big_sem, small_sem, rsend, rsem,
):
    wins = traces.shape[0]
    rows = own.shape[3]
    tiles = NF // 128
    pieces = 4 * tiles
    me = lax.axis_index("chan")
    tm = lax.axis_index("tm")
    core = lax.rem(me, 2)
    y = lax.rem(me // 2, 2)
    z = me // 4
    depth = groups // 4
    has_up = z < depth - 1
    has_down = z > 0
    has_big = jnp.where(y == 0, depth - 1 - z, z) > 0
    has_small = jnp.where(y == 0, z, depth - 1 - z) > 0
    big_base = 4 * z - 2 * y
    small_base = 4 * z - 4 + 6 * y

    def channel_start(p):
        return (p % 2) * 64 + ((p // 2) % 2) * 32 + (p // 4) * 16

    def load(p):
        return pltpu.make_async_copy(
            traces.at[:, pl.ds(pl.multiple_of(channel_start(p), 16), 16), :], tbuf.at[p], tsem.at[p]
        )

    load(0).start()
    tables = [
        pltpu.make_async_copy(source, target, fsem.at[n])
        for n, (source, target) in enumerate(((forward, fbuf), (smoother_hbm, smoother), (inverse_hbm, inverse)))
    ]
    for table in tables:
        table.start()
    for p in range(1, 8):
        load(p).start()

    barrier = pltpu.get_barrier_semaphore()
    for dz in (-1, 0, 1):
        zz = z + dz

        @pl.when((zz >= 0) & (zz < depth))
        def _():
            for k in range(4):
                for t in range(planes):

                    @pl.when((zz * 4 + k != me) | (t != tm))
                    def _():
                        pl.semaphore_signal(
                            barrier, inc=1, device_id={"chan": zz * 4 + k, "tm": t}, device_id_type=MESH
                        )

    near = 1 + has_up.astype(jnp.int32) + has_down.astype(jnp.int32)
    partners = near * (4 * planes) - 1

    for w in range(wins):
        row = mask[w : w + 1, :].astype(jnp.float32)
        maskx[w] = jnp.broadcast_to(row, (16, row.shape[1])).astype(jnp.bfloat16)

    def chunk_copies(e, c, q, act, act_local):
        src = own.at[e, c, q]
        slot = (e * 2 + c) * pieces + q
        is_big = e == y
        zt = z + 2 * e - 1
        has_z = (zt >= 0) & (zt < depth)

        def remote(dst, kind, recv, chan):
            act(
                pltpu.make_async_remote_copy(
                    src_ref=src, dst_ref=dst, send_sem=send_sem.at[slot, kind], recv_sem=recv,
                    device_id={"chan": chan}, device_id_type=MESH,
                )
            )

        @pl.when(is_big & has_z)
        def _():
            remote(big.at[q, 4 * (1 - y) + core], 0, big_sem.at[q], zt * 4 + y * 2 + c)

        @pl.when(jnp.logical_not(is_big))
        def _():
            remote(big.at[q, 2 + core], 1, big_sem.at[q], z * 4 + (1 - y) * 2 + c)

        @pl.when(jnp.logical_not(is_big) & has_z)
        def _():
            remote(small.at[q, 2 * (1 - e) + core], 0, small_sem.at[q], zt * 4 + y * 2 + c)

        @pl.when(is_big & (c != core))
        def _():
            remote(big.at[q, 4 * y + core], 2, big_sem.at[q], z * 4 + y * 2 + c)

        @pl.when(jnp.logical_not(is_big) & has_small & (c != core))
        def _():
            remote(small.at[q, 2 * (1 - y) + core], 2, small_sem.at[q], z * 4 + y * 2 + c)

        if act_local:

            @pl.when(is_big & (c == core))
            def _():
                pltpu.make_async_copy(src, big.at[q, 4 * y + core], big_sem.at[q]).start()

            @pl.when(jnp.logical_not(is_big) & has_small & (c == core))
            def _():
                pltpu.make_async_copy(src, small.at[q, 2 * (1 - y) + core], small_sem.at[q]).start()

    def start(copy):
        copy.start()

    def wait_send(copy):
        copy.wait_send()

    for table in tables:
        table.wait()

    def produce(p, carry):
        e = lax.rem(p, 2)
        c = lax.rem(p // 2, 2)
        half = p // 4
        load(p).wait()
        x = (tbuf[p] * maskx[...]).reshape(wins * 16, tbuf.shape[3])
        spectra = jnp.dot(x, fbuf[...], preferred_element_type=jnp.float32)
        real = spectra[:, :NF]
        imag = spectra[:, NF:]
        amplitude = jnp.sqrt(real * real + imag * imag)
        scaled = amplitude * jnp.float32((2 * SMOOTH + 1) * WATER / NF)
        both = jnp.concatenate([amplitude.astype(jnp.bfloat16), scaled.astype(jnp.bfloat16)], axis=1)
        total = jnp.dot(both, smoother[...], preferred_element_type=jnp.float32)
        gain = jnp.float32(2 * SMOOTH + 1) / (total + jnp.float32((2 * SMOOTH + 1) * EPS))
        for n, part in enumerate((real, imag)):
            white = (part * gain).reshape(wins, 16, NF)
            for h in range(2):
                for f in range(tiles):
                    own[e, c, (2 * half + h) * tiles + f, :, n * 128 : n * 128 + 128] = (
                        white[:, 8 * h : 8 * h + 8, f * 128 : f * 128 + 128]
                        .reshape(wins * 8, 128)
                        .astype(jnp.bfloat16)
                    )

        @pl.when(p == 0)
        def _():
            pl.semaphore_wait(barrier, partners)

        for n in range(AHEAD // 2):
            chunk_copies(e, c, half * (AHEAD // 2) + n, start, True)
        return carry

    lax.fori_loop(0, 8, produce, 0)

    def cross(buf, q, pairs, first):
        used = sorted({s for pair in pairs for s in pair})

        def step(i, sums):
            r = pl.ds(pl.multiple_of(i * 16, 16), 16)
            re = {s: buf[q, s, r, 0:128].astype(jnp.float32) for s in used}
            im = {s: buf[q, s, r, 128:256].astype(jnp.float32) for s in used}
            new = []
            for n, (a, b) in enumerate(pairs):
                direct = re[a] * re[b] + im[a] * im[b]
                crossed = re[a] * im[b] - im[a] * re[b]
                new.append(sums[2 * n] + (direct[:8] + direct[8:]))
                new.append(sums[2 * n + 1] + (crossed[:8] + crossed[8:]))
            return tuple(new)

        zero = jnp.zeros((8, 128), jnp.float32)
        sums = lax.fori_loop(0, rows // 16, step, (zero,) * (2 * len(pairs)))
        for n in range(len(pairs)):
            cross_sum[first + 8 * n : first + 8 * n + 8, 0:128] = sums[2 * n]
            cross_sum[first + 8 * n : first + 8 * n + 8, 128:256] = sums[2 * n + 1]

    def lags(f):
        value = cross_sum[...]
        high = value.astype(jnp.bfloat16)
        low = (value - high.astype(jnp.float32)).astype(jnp.bfloat16)
        return jnp.dot(
            jnp.concatenate([high, low, high], axis=1), inverse[f], preferred_element_type=jnp.float32
        ).reshape(-1, 8, LAG_PAD)

    def messages(j, base, e, first, listed, act, act_local):
        at = pl.ds(pl.multiple_of(e * 64 + core * 32 + j * 8, 8), 8)
        for k, (s, pair, count, distance) in enumerate(listed):
            chan = base + s
            src = res.at[j, pl.ds(pair, count)]
            dst = rbuf.at[tm, pl.ds(distance, count), at]
            for t in range(planes):
                mine = (chan == me) & (t == tm)

                @pl.when(jnp.logical_not(mine))
                def _():
                    act(
                        pltpu.make_async_remote_copy(
                            src_ref=src, dst_ref=dst, send_sem=rsend.at[first + k, t], recv_sem=rsem,
                            device_id={"chan": chan, "tm": t}, device_id_type=MESH,
                        )
                    )

                if act_local:

                    @pl.when(mine)
                    def _():
                        pltpu.make_async_copy(src, dst, rsem).start()

    def big_messages(j, act, act_local):
        send = functools.partial(messages, j, big_base, y, 0)

        @pl.when((y == 0) & has_big)
        def _():
            send([(0, 0, 4, 0), (1, 4, 4, 0), (2, 8, 3, 0), (3, 11, 2, 0)], act, act_local)

        @pl.when((y == 0) & jnp.logical_not(has_big))
        def _():
            send([(0, 0, 3, 0), (1, 4, 2, 0), (2, 8, 1, 0)], act, act_local)

        @pl.when((y == 1) & has_big)
        def _():
            send([(0, 1, 3, 1), (1, 4, 4, 0), (2, 8, 3, 0), (3, 11, 2, 0), (4, 13, 1, 0)], act, act_local)

        @pl.when((y == 1) & jnp.logical_not(has_big))
        def _():
            send([(2, 8, 3, 0), (3, 11, 2, 0), (4, 13, 1, 0)], act, act_local)

    def small_messages(j, act, act_local):
        @pl.when(has_small)
        def _():
            messages(j, small_base, 1 - y, 5, [(0, 14, 1, 3), (1, 15, 2, 2)], act, act_local)

    def correlate(q, carry):
        j = q // tiles
        f = lax.rem(q, tiles)

        @pl.when(has_small)
        def _():
            pltpu.make_async_copy(small.at[q], small.at[q], small_sem.at[q]).wait()

        @pl.when(has_big)
        def _():
            pltpu.make_async_copy(big.at[q], big.at[q], big_sem.at[q]).wait()

        @pl.when(jnp.logical_not(has_big))
        def _():
            there = big.at[q, pl.ds(2 * y, 4)]
            pltpu.make_async_copy(there, there, big_sem.at[q]).wait()

        @pl.when(q < pieces - AHEAD)
        def _():
            for c in range(2):
                for e in range(2):
                    chunk_copies(e, c, q + AHEAD, start, True)

        cross(big, q, BIG, 0)

        @pl.when(has_small)
        def _():
            cross(small, q, SMALL, 8 * len(BIG))

        @pl.when(f == 0)
        def _():
            res[j] = lags(f)

        @pl.when(f > 0)
        def _():
            res[j] += lags(f)

        @pl.when((f == tiles - 1) & (j > 0))
        def _():
            big_messages(j - 1, wait_send, False)
            small_messages(j - 1, wait_send, False)

        @pl.when(f == tiles - 1)
        def _():
            big_messages(j, start, True)
            small_messages(j, start, True)

        return carry

    lax.fori_loop(0, pieces, correlate, 0)
    big_messages(3, wait_send, False)
    small_messages(3, wait_send, False)

    def drain(n, carry):
        chunk_copies(n // (2 * pieces), lax.rem(n // pieces, 2), lax.rem(n, pieces), wait_send, False)
        return carry

    lax.fori_loop(0, 4 * pieces, drain, 0)

    valid = jnp.minimum(REACH, groups - 1 - me)
    for n in range(1, REACH + 1):

        @pl.when(valid == n)
        def _():
            whole = rbuf.at[:, pl.ds(0, n)]
            pltpu.make_async_copy(whole, whole, rsem).wait()

    parts = []
    for d in range(REACH):
        total = rbuf[0, d]
        for t in range(1, planes):
            total = total + rbuf[t, d]
        parts.append(total.T[:LAGS])
    for p in range(REACH):
        owner = jnp.full(parts[0].shape, owners[0, p], jnp.int32)
        picked = jnp.zeros(parts[0].shape, jnp.float32)
        for d in range(REACH):
            picked = jnp.where(owner == me + (d + 1), parts[d], picked)
        out[p] = picked


def body(traces, valid_mask, pair_owner):
    _, wins, chans, samples = traces.shape
    groups = lax.axis_size("chan")
    planes = lax.axis_size("tm")
    rows = wins * 8
    tiles = NF // 128
    pieces = 4 * tiles
    vmem = pl.BlockSpec(memory_space=pltpu.VMEM)
    hbm = pl.BlockSpec(memory_space=pl.ANY)
    f32, bf16 = jnp.float32, jnp.bfloat16
    result = pl.pallas_call(
        functools.partial(kernel, groups, planes),
        out_shape=jax.ShapeDtypeStruct((REACH, LAGS, chans), f32),
        in_specs=[hbm, vmem, pl.BlockSpec(memory_space=pltpu.SMEM), hbm, hbm, hbm],
        out_specs=vmem,
        scratch_shapes=[
            pltpu.VMEM((8, wins, 16, samples), bf16),
            pltpu.VMEM((samples, 2 * NF), bf16),
            pltpu.VMEM((2 * NF, NF), bf16),
            pltpu.VMEM((tiles, 3 * 256, LAG_PAD), bf16),
            pltpu.VMEM((wins, 16, samples), bf16),
            pltpu.VMEM((2, 2, pieces, rows, 256), bf16),
            pltpu.VMEM((pieces, 6, rows, 256), bf16),
            pltpu.VMEM((pieces, 4, rows, 256), bf16),
            pltpu.VMEM(((len(BIG) + len(SMALL)) * 8, 256), f32),
            pltpu.VMEM((4, len(BIG) + len(SMALL), 8, LAG_PAD), f32),
            pltpu.VMEM((planes, REACH, chans, LAG_PAD), f32),
            pltpu.SemaphoreType.DMA((8,)),
            pltpu.SemaphoreType.DMA((3,)),
            pltpu.SemaphoreType.DMA((4 * pieces, 3)),
            pltpu.SemaphoreType.DMA((pieces,)),
            pltpu.SemaphoreType.DMA((pieces,)),
            pltpu.SemaphoreType.DMA((7, planes)),
            pltpu.SemaphoreType.DMA,
        ],
        compiler_params=pltpu.CompilerParams(
            collective_id=0, has_side_effects=True, vmem_limit_bytes=56 * 1024 * 1024
        ),
        name="correlate",
    )(
        traces[0],
        valid_mask[0],
        pair_owner,
        jnp.asarray(forward_table(samples)),
        jnp.asarray(smooth_table()),
        jnp.asarray(inverse_table(samples, wins * planes)),
    )
    return result[None]


def solution(mesh):
    return jax.shard_map(
        body,
        mesh=mesh,
        in_specs=(P("chan", "tm", None, None), P("chan", "tm", None), P("chan", None)),
        out_specs=P("chan", None, None, None),
        check_vma=False,
    )
```

```python
import functools
import math

import jax
import jax.numpy as jnp
import ml_dtypes
import numpy as np
from jax import lax
from jax.experimental import pallas as pl
from jax.experimental.pallas import tpu as pltpu
from jax.sharding import PartitionSpec as P

NF = 256
MAXLAG = 50
LAGS = 2 * MAXLAG + 1
SMOOTH = 4
REACH = 4
LAG_PAD = 128
AHEAD = 4

WATER = 0.05
EPS = 1e-06

MESH = pl.DeviceIdType.MESH

BIG = [
    (0, 1), (0, 2), (0, 3), (0, 4),
    (1, 2), (1, 3), (1, 4), (1, 5),
    (2, 3), (2, 4), (2, 5),
    (3, 4), (3, 5),
    (4, 5),
]
SMALL = [(0, 2), (1, 2), (1, 3)]


def forward_table(samples_count):
    samples = np.arange(samples_count)
    bins = np.arange(1, NF + 1)
    angle = (samples[:, None] * bins[None, :] % samples_count) * (2.0 * math.pi / samples_count)
    return np.concatenate([np.cos(angle), -np.sin(angle)], axis=1).astype(ml_dtypes.bfloat16)


def inverse_table(samples_count, windows_all):
    bins = np.arange(1, NF + 1)
    offsets = np.arange(LAGS) - MAXLAG
    angle = (bins[:, None] * offsets[None, :] % samples_count) * (2.0 * math.pi / samples_count)
    table = np.concatenate([np.cos(angle), -np.sin(angle)], axis=0) / math.sqrt(windows_all * NF)
    table = np.pad(table, ((0, 0), (0, LAG_PAD - LAGS))).astype(np.float32)
    high = table.astype(ml_dtypes.bfloat16)
    low = (table - high.astype(np.float32)).astype(ml_dtypes.bfloat16)
    tiles = NF // 128
    parts = []
    for f in range(tiles):
        picked = np.concatenate([np.arange(f * 128, f * 128 + 128), np.arange(NF + f * 128, NF + f * 128 + 128)])
        parts.append(np.concatenate([high[picked], high[picked], low[picked]], axis=0))
    return np.stack(parts)


def smooth_table():
    bins = np.arange(NF)
    band = (np.abs(bins[:, None] - bins[None, :]) <= SMOOTH).astype(np.float32)
    return np.concatenate([band, np.ones((NF, NF), np.float32)], axis=0).astype(ml_dtypes.bfloat16)


def kernel(
    groups, planes,
    traces, mask, owners, forward, smoother_hbm, inverse_hbm,
    out,
    tbuf, fbuf, smoother, inverse, maskx, own, big, small, cross_sum, res, packed, rbuf,
    tsem, fsem, send_sem, big_sem, small_sem, rsend, rsem,
):
    wins = traces.shape[0]
    rows = own.shape[3]
    tiles = NF // 128
    pieces = 4 * tiles
    me = lax.axis_index("chan")
    tm = lax.axis_index("tm")
    core = lax.rem(me, 2)
    y = lax.rem(me // 2, 2)
    z = me // 4
    depth = groups // 4
    has_up = z < depth - 1
    has_down = z > 0
    has_big = jnp.where(y == 0, depth - 1 - z, z) > 0
    has_small = jnp.where(y == 0, z, depth - 1 - z) > 0
    big_base = 4 * z - 2 * y
    small_base = 4 * z - 4 + 6 * y

    def channel_start(p):
        return (p % 2) * 64 + ((p // 2) % 2) * 32 + (p // 4) * 16

    def load(p):
        return pltpu.make_async_copy(
            traces.at[:, pl.ds(pl.multiple_of(channel_start(p), 16), 16), :], tbuf.at[p], tsem.at[p]
        )

    load(0).start()
    tables = [
        pltpu.make_async_copy(source, target, fsem.at[n])
        for n, (source, target) in enumerate(((forward, fbuf), (smoother_hbm, smoother), (inverse_hbm, inverse)))
    ]
    for table in tables:
        table.start()
    for p in range(1, 8):
        load(p).start()

    barrier = pltpu.get_barrier_semaphore()
    for dz in (-1, 0, 1):
        zz = z + dz

        @pl.when((zz >= 0) & (zz < depth))
        def _():
            for k in range(4):
                for t in range(planes):

                    @pl.when((zz * 4 + k != me) | (t != tm))
                    def _():
                        pl.semaphore_signal(
                            barrier, inc=1, device_id={"chan": zz * 4 + k, "tm": t}, device_id_type=MESH
                        )

    near = 1 + has_up.astype(jnp.int32) + has_down.astype(jnp.int32)
    partners = near * (4 * planes) - 1

    for w in range(wins):
        row = mask[w : w + 1, :].astype(jnp.float32)
        maskx[w] = jnp.broadcast_to(row, (16, row.shape[1])).astype(jnp.bfloat16)

    def chunk_copies(e, c, q, act, act_local):
        src = own.at[e, c, q]
        slot = (e * 2 + c) * pieces + q
        is_big = e == y
        zt = z + 2 * e - 1
        has_z = (zt >= 0) & (zt < depth)

        def remote(dst, kind, recv, chan):
            act(
                pltpu.make_async_remote_copy(
                    src_ref=src, dst_ref=dst, send_sem=send_sem.at[slot, kind], recv_sem=recv,
                    device_id={"chan": chan}, device_id_type=MESH,
                )
            )

        @pl.when(is_big & has_z)
        def _():
            remote(big.at[q, 4 * (1 - y) + core], 0, big_sem.at[q], zt * 4 + y * 2 + c)

        @pl.when(jnp.logical_not(is_big))
        def _():
            remote(big.at[q, 2 + core], 1, big_sem.at[q], z * 4 + (1 - y) * 2 + c)

        @pl.when(jnp.logical_not(is_big) & has_z)
        def _():
            remote(small.at[q, 2 * (1 - e) + core], 0, small_sem.at[q], zt * 4 + y * 2 + c)

        @pl.when(is_big & (c != core))
        def _():
            remote(big.at[q, 4 * y + core], 2, big_sem.at[q], z * 4 + y * 2 + c)

        @pl.when(jnp.logical_not(is_big) & has_small & (c != core))
        def _():
            remote(small.at[q, 2 * (1 - y) + core], 2, small_sem.at[q], z * 4 + y * 2 + c)

        if act_local:

            @pl.when(is_big & (c == core))
            def _():
                pltpu.make_async_copy(src, big.at[q, 4 * y + core], big_sem.at[q]).start()

            @pl.when(jnp.logical_not(is_big) & has_small & (c == core))
            def _():
                pltpu.make_async_copy(src, small.at[q, 2 * (1 - y) + core], small_sem.at[q]).start()

    def start(copy):
        copy.start()

    def wait_send(copy):
        copy.wait_send()

    for table in tables:
        table.wait()

    def produce(p, carry):
        e = lax.rem(p, 2)
        c = lax.rem(p // 2, 2)
        half = p // 4
        load(p).wait()
        x = (tbuf[p] * maskx[...]).reshape(wins * 16, tbuf.shape[3])
        spectra = jnp.dot(x, fbuf[...], preferred_element_type=jnp.float32)
        real = spectra[:, :NF]
        imag = spectra[:, NF:]
        amplitude = jnp.sqrt(real * real + imag * imag)
        scaled = amplitude * jnp.float32((2 * SMOOTH + 1) * WATER / NF)
        both = jnp.concatenate([amplitude.astype(jnp.bfloat16), scaled.astype(jnp.bfloat16)], axis=1)
        total = jnp.dot(both, smoother[...], preferred_element_type=jnp.float32)
        gain = jnp.float32(2 * SMOOTH + 1) / (total + jnp.float32((2 * SMOOTH + 1) * EPS))
        for n, part in enumerate((real, imag)):
            white = (part * gain).reshape(wins, 16, NF)
            for h in range(2):
                for f in range(tiles):
                    own[e, c, (2 * half + h) * tiles + f, :, n * 128 : n * 128 + 128] = (
                        white[:, 8 * h : 8 * h + 8, f * 128 : f * 128 + 128]
                        .reshape(wins * 8, 128)
                        .astype(jnp.bfloat16)
                    )

        @pl.when(p == 0)
        def _():
            pl.semaphore_wait(barrier, partners)

        for n in range(AHEAD // 2):
            chunk_copies(e, c, half * (AHEAD // 2) + n, start, True)
        return carry

    lax.fori_loop(0, 8, produce, 0)

    def cross(buf, q, pairs, first):
        used = sorted({s for pair in pairs for s in pair})

        def step(i, sums):
            r = pl.ds(pl.multiple_of(i * 16, 16), 16)
            re = {s: buf[q, s, r, 0:128].astype(jnp.float32) for s in used}
            im = {s: buf[q, s, r, 128:256].astype(jnp.float32) for s in used}
            new = []
            for n, (a, b) in enumerate(pairs):
                direct = re[a] * re[b] + im[a] * im[b]
                crossed = re[a] * im[b] - im[a] * re[b]
                new.append(sums[2 * n] + (direct[:8] + direct[8:]))
                new.append(sums[2 * n + 1] + (crossed[:8] + crossed[8:]))
            return tuple(new)

        zero = jnp.zeros((8, 128), jnp.float32)
        sums = lax.fori_loop(0, rows // 16, step, (zero,) * (2 * len(pairs)))
        for n in range(len(pairs)):
            cross_sum[first + 8 * n : first + 8 * n + 8, 0:128] = sums[2 * n]
            cross_sum[first + 8 * n : first + 8 * n + 8, 128:256] = sums[2 * n + 1]

    def lags(f):
        value = cross_sum[...]
        high = value.astype(jnp.bfloat16)
        low = (value - high.astype(jnp.float32)).astype(jnp.bfloat16)
        return jnp.dot(
            jnp.concatenate([high, low, high], axis=1), inverse[f], preferred_element_type=jnp.float32
        ).reshape(-1, 8, LAG_PAD)

    def messages(j, base, e, first, listed, act, act_local):
        at = pl.ds(pl.multiple_of(e * 64 + core * 32 + j * 16, 16), 16)
        for k, (s, pair, count, distance) in enumerate(listed):
            chan = base + s
            src = packed.at[j, pl.ds(pair, count)]
            dst = rbuf.at[tm, pl.ds(distance, count), at]
            for t in range(planes):
                mine = (chan == me) & (t == tm)

                @pl.when(jnp.logical_not(mine))
                def _():
                    act(
                        pltpu.make_async_remote_copy(
                            src_ref=src, dst_ref=dst, send_sem=rsend.at[first + k, t], recv_sem=rsem,
                            device_id={"chan": chan, "tm": t}, device_id_type=MESH,
                        )
                    )

                if act_local:

                    @pl.when(mine)
                    def _():
                        pltpu.make_async_copy(src, dst, rsem).start()

    def big_messages(j, act, act_local):
        send = functools.partial(messages, j, big_base, y, 0)

        @pl.when((y == 0) & has_big)
        def _():
            send([(0, 0, 4, 0), (1, 4, 4, 0), (2, 8, 3, 0), (3, 11, 2, 0)], act, act_local)

        @pl.when((y == 0) & jnp.logical_not(has_big))
        def _():
            send([(0, 0, 3, 0), (1, 4, 2, 0), (2, 8, 1, 0)], act, act_local)

        @pl.when((y == 1) & has_big)
        def _():
            send([(0, 1, 3, 1), (1, 4, 4, 0), (2, 8, 3, 0), (3, 11, 2, 0), (4, 13, 1, 0)], act, act_local)

        @pl.when((y == 1) & jnp.logical_not(has_big))
        def _():
            send([(2, 8, 3, 0), (3, 11, 2, 0), (4, 13, 1, 0)], act, act_local)

    def small_messages(j, act, act_local):
        @pl.when(has_small)
        def _():
            messages(j, small_base, 1 - y, 5, [(0, 14, 1, 3), (1, 15, 2, 2)], act, act_local)

    def correlate(q, carry):
        j = q // tiles
        f = lax.rem(q, tiles)

        @pl.when(has_small)
        def _():
            pltpu.make_async_copy(small.at[q], small.at[q], small_sem.at[q]).wait()

        @pl.when(has_big)
        def _():
            pltpu.make_async_copy(big.at[q], big.at[q], big_sem.at[q]).wait()

        @pl.when(jnp.logical_not(has_big))
        def _():
            there = big.at[q, pl.ds(2 * y, 4)]
            pltpu.make_async_copy(there, there, big_sem.at[q]).wait()

        @pl.when(q < pieces - AHEAD)
        def _():
            for c in range(2):
                for e in range(2):
                    chunk_copies(e, c, q + AHEAD, start, True)

        cross(big, q, BIG, 0)

        @pl.when(has_small)
        def _():
            cross(small, q, SMALL, 8 * len(BIG))

        h = lax.rem(j, 2)

        @pl.when(f == 0)
        def _():
            res[h] = lags(f)

        @pl.when(f > 0)
        def _():
            res[h] += lags(f)

        last = (f == tiles - 1) & (h == 1)

        @pl.when(last & (j > 1))
        def _():
            big_messages(0, wait_send, False)
            small_messages(0, wait_send, False)

        @pl.when(last)
        def _():
            packed[j // 2] = jnp.concatenate([res[0], res[1]], axis=1).astype(jnp.bfloat16)
            big_messages(j // 2, start, True)
            small_messages(j // 2, start, True)

        return carry

    lax.fori_loop(0, pieces, correlate, 0)
    big_messages(1, wait_send, False)
    small_messages(1, wait_send, False)

    def drain(n, carry):
        chunk_copies(n // (2 * pieces), lax.rem(n // pieces, 2), lax.rem(n, pieces), wait_send, False)
        return carry

    lax.fori_loop(0, 4 * pieces, drain, 0)

    valid = jnp.minimum(REACH, groups - 1 - me)
    for n in range(1, REACH + 1):

        @pl.when(valid == n)
        def _():
            whole = rbuf.at[:, pl.ds(0, n)]
            pltpu.make_async_copy(whole, whole, rsem).wait()

    parts = []
    for d in range(REACH):
        total = rbuf[0, d].astype(jnp.float32)
        for t in range(1, planes):
            total = total + rbuf[t, d].astype(jnp.float32)
        parts.append(total.T[:LAGS])
    for p in range(REACH):
        owner = jnp.full(parts[0].shape, owners[0, p], jnp.int32)
        picked = jnp.zeros(parts[0].shape, jnp.float32)
        for d in range(REACH):
            picked = jnp.where(owner == me + (d + 1), parts[d], picked)
        out[:, p, :] = picked


def body(traces, valid_mask, pair_owner):
    _, wins, chans, samples = traces.shape
    groups = lax.axis_size("chan")
    planes = lax.axis_size("tm")
    rows = wins * 8
    tiles = NF // 128
    pieces = 4 * tiles
    vmem = pl.BlockSpec(memory_space=pltpu.VMEM)
    hbm = pl.BlockSpec(memory_space=pl.ANY)
    f32, bf16 = jnp.float32, jnp.bfloat16
    result = pl.pallas_call(
        functools.partial(kernel, groups, planes),
        out_shape=jax.ShapeDtypeStruct((LAGS, REACH, chans), f32),
        in_specs=[hbm, vmem, pl.BlockSpec(memory_space=pltpu.SMEM), hbm, hbm, hbm],
        out_specs=vmem,
        scratch_shapes=[
            pltpu.VMEM((8, wins, 16, samples), bf16),
            pltpu.VMEM((samples, 2 * NF), bf16),
            pltpu.VMEM((2 * NF, NF), bf16),
            pltpu.VMEM((tiles, 3 * 256, LAG_PAD), bf16),
            pltpu.VMEM((wins, 16, samples), bf16),
            pltpu.VMEM((2, 2, pieces, rows, 256), bf16),
            pltpu.VMEM((pieces, 6, rows, 256), bf16),
            pltpu.VMEM((pieces, 4, rows, 256), bf16),
            pltpu.VMEM(((len(BIG) + len(SMALL)) * 8, 256), f32),
            pltpu.VMEM((2, len(BIG) + len(SMALL), 8, LAG_PAD), f32),
            pltpu.VMEM((2, len(BIG) + len(SMALL), 16, LAG_PAD), bf16),
            pltpu.VMEM((planes, REACH, chans, LAG_PAD), bf16),
            pltpu.SemaphoreType.DMA((8,)),
            pltpu.SemaphoreType.DMA((3,)),
            pltpu.SemaphoreType.DMA((4 * pieces, 3)),
            pltpu.SemaphoreType.DMA((pieces,)),
            pltpu.SemaphoreType.DMA((pieces,)),
            pltpu.SemaphoreType.DMA((7, planes)),
            pltpu.SemaphoreType.DMA,
        ],
        compiler_params=pltpu.CompilerParams(
            collective_id=0, has_side_effects=True, vmem_limit_bytes=56 * 1024 * 1024
        ),
        name="correlate",
    )(
        traces[0],
        valid_mask[0],
        pair_owner,
        jnp.asarray(forward_table(samples)),
        jnp.asarray(smooth_table()),
        jnp.asarray(inverse_table(samples, wins * planes)),
    )
    return result.transpose(1, 0, 2)[None]


def solution(mesh):
    return jax.shard_map(
        body,
        mesh=mesh,
        in_specs=(P("chan", "tm", None, None), P("chan", "tm", None), P("chan", None)),
        out_specs=P("chan", None, None, None),
        check_vma=False,
    )
```

```python
import functools
import math

import jax
import jax.numpy as jnp
import ml_dtypes
import numpy as np
from jax import lax
from jax.experimental import pallas as pl
from jax.experimental.pallas import tpu as pltpu
from jax.sharding import PartitionSpec as P

NF = 256
MAXLAG = 50
LAGS = 2 * MAXLAG + 1
SMOOTH = 4
REACH = 4
LAG_PAD = 128
AHEAD = 2

WATER = 0.05
EPS = 1e-06

MESH = pl.DeviceIdType.MESH

BIG = [
    (0, 1), (0, 2), (0, 3), (0, 4),
    (1, 2), (1, 3), (1, 4), (1, 5),
    (2, 3), (2, 4), (2, 5),
    (3, 4), (3, 5),
    (4, 5),
]
SMALL = [(0, 2), (1, 2), (1, 3)]


def forward_table(samples_count):
    samples = np.arange(samples_count)
    bins = np.arange(1, NF + 1)
    angle = (samples[:, None] * bins[None, :] % samples_count) * (2.0 * math.pi / samples_count)
    return np.concatenate([np.cos(angle), -np.sin(angle)], axis=1).astype(ml_dtypes.bfloat16)


def inverse_table(samples_count, windows_all):
    bins = np.arange(1, NF + 1)
    offsets = np.arange(LAGS) - MAXLAG
    angle = (bins[:, None] * offsets[None, :] % samples_count) * (2.0 * math.pi / samples_count)
    table = np.concatenate([np.cos(angle), -np.sin(angle)], axis=0) / math.sqrt(windows_all * NF)
    table = np.pad(table, ((0, 0), (0, LAG_PAD - LAGS))).astype(np.float32)
    high = table.astype(ml_dtypes.bfloat16)
    low = (table - high.astype(np.float32)).astype(ml_dtypes.bfloat16)
    tiles = NF // 128
    parts = []
    for f in range(tiles):
        picked = np.concatenate([np.arange(f * 128, f * 128 + 128), np.arange(NF + f * 128, NF + f * 128 + 128)])
        parts.append(np.concatenate([high[picked], high[picked], low[picked]], axis=0))
    return np.stack(parts)


def smooth_table():
    bins = np.arange(NF)
    band = (np.abs(bins[:, None] - bins[None, :]) <= SMOOTH).astype(np.float32)
    return np.concatenate([band, np.ones((NF, NF), np.float32)], axis=0).astype(ml_dtypes.bfloat16)


def kernel(
    groups, planes,
    traces, mask, owners, forward, smoother_hbm, inverse_hbm,
    out,
    tbuf, fbuf, smoother, inverse, maskx, own, big, small, cross_sum, res, packed, rbuf,
    tsem, fsem, send_sem, big_sem, small_sem, rsend, rsem,
):
    wins = traces.shape[0]
    rows = own.shape[3]
    tiles = NF // 128
    pieces = 4 * tiles
    me = lax.axis_index("chan")
    tm = lax.axis_index("tm")
    core = lax.rem(me, 2)
    y = lax.rem(me // 2, 2)
    z = me // 4
    depth = groups // 4
    has_up = z < depth - 1
    has_down = z > 0
    has_big = jnp.where(y == 0, depth - 1 - z, z) > 0
    has_small = jnp.where(y == 0, z, depth - 1 - z) > 0
    big_base = 4 * z - 2 * y
    small_base = 4 * z - 4 + 6 * y

    def channel_start(p):
        return (p % 2) * 64 + ((p // 2) % 2) * 32 + (p // 4) * 16

    def load(p):
        return pltpu.make_async_copy(
            traces.at[:, pl.ds(pl.multiple_of(channel_start(p), 16), 16), :], tbuf.at[p], tsem.at[p]
        )

    load(0).start()
    tables = [
        pltpu.make_async_copy(source, target, fsem.at[n])
        for n, (source, target) in enumerate(((forward, fbuf), (smoother_hbm, smoother), (inverse_hbm, inverse)))
    ]
    for table in tables:
        table.start()
    for p in range(1, 8):
        load(p).start()

    barrier = pltpu.get_barrier_semaphore()
    for dz in (-1, 0, 1):
        zz = z + dz

        @pl.when((zz >= 0) & (zz < depth))
        def _():
            for k in range(4):
                for t in range(planes):

                    @pl.when((zz * 4 + k != me) | (t != tm))
                    def _():
                        pl.semaphore_signal(
                            barrier, inc=1, device_id={"chan": zz * 4 + k, "tm": t}, device_id_type=MESH
                        )

    near = 1 + has_up.astype(jnp.int32) + has_down.astype(jnp.int32)
    partners = near * (4 * planes) - 1

    for w in range(wins):
        row = mask[w : w + 1, :].astype(jnp.float32)
        maskx[w] = jnp.broadcast_to(row, (16, row.shape[1])).astype(jnp.bfloat16)

    def chunk_copies(e, c, q, act, act_local):
        src = own.at[e, c, q]
        slot = (e * 2 + c) * pieces + q
        is_big = e == y
        zt = z + 2 * e - 1
        has_z = (zt >= 0) & (zt < depth)

        def remote(dst, kind, recv, chan):
            act(
                pltpu.make_async_remote_copy(
                    src_ref=src, dst_ref=dst, send_sem=send_sem.at[slot, kind], recv_sem=recv,
                    device_id={"chan": chan}, device_id_type=MESH,
                )
            )

        @pl.when(is_big & has_z)
        def _():
            remote(big.at[q, 4 * (1 - y) + core], 0, big_sem.at[q], zt * 4 + y * 2 + c)

        @pl.when(jnp.logical_not(is_big))
        def _():
            remote(big.at[q, 2 + core], 1, big_sem.at[q], z * 4 + (1 - y) * 2 + c)

        @pl.when(jnp.logical_not(is_big) & has_z)
        def _():
            remote(small.at[q, 2 * (1 - e) + core], 0, small_sem.at[q], zt * 4 + y * 2 + c)

        @pl.when(is_big & (c != core))
        def _():
            remote(big.at[q, 4 * y + core], 2, big_sem.at[q], z * 4 + y * 2 + c)

        @pl.when(jnp.logical_not(is_big) & has_small & (c != core))
        def _():
            remote(small.at[q, 2 * (1 - y) + core], 2, small_sem.at[q], z * 4 + y * 2 + c)

        if act_local:

            @pl.when(is_big & (c == core))
            def _():
                pltpu.make_async_copy(src, big.at[q, 4 * y + core], big_sem.at[q]).start()

            @pl.when(jnp.logical_not(is_big) & has_small & (c == core))
            def _():
                pltpu.make_async_copy(src, small.at[q, 2 * (1 - y) + core], small_sem.at[q]).start()

    def start(copy):
        copy.start()

    def wait_send(copy):
        copy.wait_send()

    for table in tables:
        table.wait()

    def produce(p, carry):
        e = lax.rem(p, 2)
        c = lax.rem(p // 2, 2)
        half = p // 4
        load(p).wait()
        x = (tbuf[p] * maskx[...]).reshape(wins * 16, tbuf.shape[3])
        spectra = jnp.dot(x, fbuf[...], preferred_element_type=jnp.float32)
        real = spectra[:, :NF]
        imag = spectra[:, NF:]
        amplitude = jnp.sqrt(real * real + imag * imag)
        scaled = amplitude * jnp.float32((2 * SMOOTH + 1) * WATER / NF)
        both = jnp.concatenate([amplitude.astype(jnp.bfloat16), scaled.astype(jnp.bfloat16)], axis=1)
        total = jnp.dot(both, smoother[...], preferred_element_type=jnp.float32)
        gain = jnp.float32(2 * SMOOTH + 1) / (total + jnp.float32((2 * SMOOTH + 1) * EPS))
        for n, part in enumerate((real, imag)):
            white = (part * gain).reshape(wins, 16, NF)
            for h in range(2):
                for f in range(tiles):
                    own[e, c, (2 * half + h) * tiles + f, :, n * 128 : n * 128 + 128] = (
                        white[:, 8 * h : 8 * h + 8, f * 128 : f * 128 + 128]
                        .reshape(wins * 8, 128)
                        .astype(jnp.bfloat16)
                    )

        @pl.when(p == 0)
        def _():
            pl.semaphore_wait(barrier, partners)

        for n in range(AHEAD // 2):
            chunk_copies(e, c, half * (AHEAD // 2) + n, start, True)
        return carry

    lax.fori_loop(0, 8, produce, 0)

    def cross(buf, q, pairs, first):
        used = sorted({s for pair in pairs for s in pair})

        def step(i, sums):
            r = pl.ds(pl.multiple_of(i * 16, 16), 16)
            re = {s: buf[q, s, r, 0:128].astype(jnp.float32) for s in used}
            im = {s: buf[q, s, r, 128:256].astype(jnp.float32) for s in used}
            new = []
            for n, (a, b) in enumerate(pairs):
                direct = re[a] * re[b] + im[a] * im[b]
                crossed = re[a] * im[b] - im[a] * re[b]
                new.append(sums[2 * n] + (direct[:8] + direct[8:]))
                new.append(sums[2 * n + 1] + (crossed[:8] + crossed[8:]))
            return tuple(new)

        zero = jnp.zeros((8, 128), jnp.float32)
        sums = lax.fori_loop(0, rows // 16, step, (zero,) * (2 * len(pairs)))
        for n in range(len(pairs)):
            cross_sum[first + 8 * n : first + 8 * n + 8, 0:128] = sums[2 * n]
            cross_sum[first + 8 * n : first + 8 * n + 8, 128:256] = sums[2 * n + 1]

    def lags(f):
        value = cross_sum[...]
        high = value.astype(jnp.bfloat16)
        low = (value - high.astype(jnp.float32)).astype(jnp.bfloat16)
        return jnp.dot(
            jnp.concatenate([high, low, high], axis=1), inverse[f], preferred_element_type=jnp.float32
        ).reshape(-1, 8, LAG_PAD)

    def messages(j, base, e, first, listed, act, act_local):
        at = pl.ds(pl.multiple_of(e * 64 + core * 32 + j * 16, 16), 16)
        for k, (s, pair, count, distance) in enumerate(listed):
            chan = base + s
            src = packed.at[j, pl.ds(pair, count)]
            dst = rbuf.at[tm, pl.ds(distance, count), at]
            for t in range(planes):
                mine = (chan == me) & (t == tm)

                @pl.when(jnp.logical_not(mine))
                def _():
                    act(
                        pltpu.make_async_remote_copy(
                            src_ref=src, dst_ref=dst, send_sem=rsend.at[first + k, t], recv_sem=rsem,
                            device_id={"chan": chan, "tm": t}, device_id_type=MESH,
                        )
                    )

                if act_local:

                    @pl.when(mine)
                    def _():
                        pltpu.make_async_copy(src, dst, rsem).start()

    def big_messages(j, act, act_local):
        send = functools.partial(messages, j, big_base, y, 0)

        @pl.when((y == 0) & has_big)
        def _():
            send([(0, 0, 4, 0), (1, 4, 4, 0), (2, 8, 3, 0), (3, 11, 2, 0)], act, act_local)

        @pl.when((y == 0) & jnp.logical_not(has_big))
        def _():
            send([(0, 0, 3, 0), (1, 4, 2, 0), (2, 8, 1, 0)], act, act_local)

        @pl.when((y == 1) & has_big)
        def _():
            send([(0, 1, 3, 1), (1, 4, 4, 0), (2, 8, 3, 0), (3, 11, 2, 0), (4, 13, 1, 0)], act, act_local)

        @pl.when((y == 1) & jnp.logical_not(has_big))
        def _():
            send([(2, 8, 3, 0), (3, 11, 2, 0), (4, 13, 1, 0)], act, act_local)

    def small_messages(j, act, act_local):
        @pl.when(has_small)
        def _():
            messages(j, small_base, 1 - y, 5, [(0, 14, 1, 3), (1, 15, 2, 2)], act, act_local)

    def correlate(q, carry):
        j = q // tiles
        f = lax.rem(q, tiles)

        @pl.when(has_small)
        def _():
            pltpu.make_async_copy(small.at[q], small.at[q], small_sem.at[q]).wait()

        @pl.when(has_big)
        def _():
            pltpu.make_async_copy(big.at[q], big.at[q], big_sem.at[q]).wait()

        @pl.when(jnp.logical_not(has_big))
        def _():
            there = big.at[q, pl.ds(2 * y, 4)]
            pltpu.make_async_copy(there, there, big_sem.at[q]).wait()

        @pl.when(q < pieces - AHEAD)
        def _():
            for c in range(2):
                for e in range(2):
                    chunk_copies(e, c, q + AHEAD, start, True)

        cross(big, q, BIG, 0)

        @pl.when(has_small)
        def _():
            cross(small, q, SMALL, 8 * len(BIG))

        h = lax.rem(j, 2)

        @pl.when(f == 0)
        def _():
            res[h] = lags(f)

        @pl.when(f > 0)
        def _():
            res[h] += lags(f)

        last = (f == tiles - 1) & (h == 1)

        @pl.when(last & (j > 1))
        def _():
            big_messages(0, wait_send, False)
            small_messages(0, wait_send, False)

        @pl.when(last)
        def _():
            packed[j // 2] = jnp.concatenate([res[0], res[1]], axis=1).astype(jnp.bfloat16)
            big_messages(j // 2, start, True)
            small_messages(j // 2, start, True)

        return carry

    lax.fori_loop(0, pieces, correlate, 0)
    big_messages(1, wait_send, False)
    small_messages(1, wait_send, False)

    def drain(n, carry):
        chunk_copies(n // (2 * pieces), lax.rem(n // pieces, 2), lax.rem(n, pieces), wait_send, False)
        return carry

    lax.fori_loop(0, 4 * pieces, drain, 0)

    valid = jnp.minimum(REACH, groups - 1 - me)
    for n in range(1, REACH + 1):

        @pl.when(valid == n)
        def _():
            whole = rbuf.at[:, pl.ds(0, n)]
            pltpu.make_async_copy(whole, whole, rsem).wait()

    parts = []
    for d in range(REACH):
        total = rbuf[0, d].astype(jnp.float32)
        for t in range(1, planes):
            total = total + rbuf[t, d].astype(jnp.float32)
        parts.append(total.T[:LAGS])
    for p in range(REACH):
        owner = jnp.full(parts[0].shape, owners[0, p], jnp.int32)
        picked = jnp.zeros(parts[0].shape, jnp.float32)
        for d in range(REACH):
            picked = jnp.where(owner == me + (d + 1), parts[d], picked)
        out[:, p, :] = picked


def body(traces, valid_mask, pair_owner):
    _, wins, chans, samples = traces.shape
    groups = lax.axis_size("chan")
    planes = lax.axis_size("tm")
    rows = wins * 8
    tiles = NF // 128
    pieces = 4 * tiles
    vmem = pl.BlockSpec(memory_space=pltpu.VMEM)
    hbm = pl.BlockSpec(memory_space=pl.ANY)
    f32, bf16 = jnp.float32, jnp.bfloat16
    result = pl.pallas_call(
        functools.partial(kernel, groups, planes),
        out_shape=jax.ShapeDtypeStruct((LAGS, REACH, chans), f32),
        in_specs=[hbm, vmem, pl.BlockSpec(memory_space=pltpu.SMEM), hbm, hbm, hbm],
        out_specs=vmem,
        scratch_shapes=[
            pltpu.VMEM((8, wins, 16, samples), bf16),
            pltpu.VMEM((samples, 2 * NF), bf16),
            pltpu.VMEM((2 * NF, NF), bf16),
            pltpu.VMEM((tiles, 3 * 256, LAG_PAD), bf16),
            pltpu.VMEM((wins, 16, samples), bf16),
            pltpu.VMEM((2, 2, pieces, rows, 256), bf16),
            pltpu.VMEM((pieces, 6, rows, 256), bf16),
            pltpu.VMEM((pieces, 4, rows, 256), bf16),
            pltpu.VMEM(((len(BIG) + len(SMALL)) * 8, 256), f32),
            pltpu.VMEM((2, len(BIG) + len(SMALL), 8, LAG_PAD), f32),
            pltpu.VMEM((2, len(BIG) + len(SMALL), 16, LAG_PAD), bf16),
            pltpu.VMEM((planes, REACH, chans, LAG_PAD), bf16),
            pltpu.SemaphoreType.DMA((8,)),
            pltpu.SemaphoreType.DMA((3,)),
            pltpu.SemaphoreType.DMA((4 * pieces, 3)),
            pltpu.SemaphoreType.DMA((pieces,)),
            pltpu.SemaphoreType.DMA((pieces,)),
            pltpu.SemaphoreType.DMA((7, planes)),
            pltpu.SemaphoreType.DMA,
        ],
        compiler_params=pltpu.CompilerParams(
            collective_id=0, has_side_effects=True, vmem_limit_bytes=56 * 1024 * 1024
        ),
        name="correlate",
    )(
        traces[0],
        valid_mask[0],
        pair_owner,
        jnp.asarray(forward_table(samples)),
        jnp.asarray(smooth_table()),
        jnp.asarray(inverse_table(samples, wins * planes)),
    )
    return result.transpose(1, 0, 2)[None]


def solution(mesh):
    return jax.shard_map(
        body,
        mesh=mesh,
        in_specs=(P("chan", "tm", None, None), P("chan", "tm", None), P("chan", None)),
        out_specs=P("chan", None, None, None),
        check_vma=False,
    )
```

```python
import functools
import math

import jax
import jax.numpy as jnp
import ml_dtypes
import numpy as np
from jax import lax
from jax.experimental import pallas as pl
from jax.experimental.pallas import tpu as pltpu
from jax.sharding import PartitionSpec as P

NF = 256
MAXLAG = 50
LAGS = 2 * MAXLAG + 1
SMOOTH = 4
REACH = 4
LAG_PAD = 128
AHEAD = 4

WATER = 0.05
EPS = 1e-06

MESH = pl.DeviceIdType.MESH

BIG = [
    (0, 1), (0, 2), (0, 3), (0, 4),
    (1, 2), (1, 3), (1, 4), (1, 5),
    (2, 3), (2, 4), (2, 5),
    (3, 4), (3, 5),
    (4, 5),
]
SMALL = [(0, 2), (1, 2), (1, 3)]


def forward_table(samples_count):
    samples = np.arange(samples_count)
    bins = np.arange(1, NF + 1)
    angle = (samples[:, None] * bins[None, :] % samples_count) * (2.0 * math.pi / samples_count)
    return np.concatenate([np.cos(angle), -np.sin(angle)], axis=1).astype(ml_dtypes.bfloat16)


def inverse_table(samples_count, windows_all):
    bins = np.arange(1, NF + 1)
    offsets = np.arange(LAGS) - MAXLAG
    angle = (bins[:, None] * offsets[None, :] % samples_count) * (2.0 * math.pi / samples_count)
    table = np.concatenate([np.cos(angle), -np.sin(angle)], axis=0) / math.sqrt(windows_all * NF)
    table = np.pad(table, ((0, 0), (0, LAG_PAD - LAGS))).astype(np.float32)
    high = table.astype(ml_dtypes.bfloat16)
    low = (table - high.astype(np.float32)).astype(ml_dtypes.bfloat16)
    tiles = NF // 128
    parts = []
    for f in range(tiles):
        picked = np.concatenate([np.arange(f * 128, f * 128 + 128), np.arange(NF + f * 128, NF + f * 128 + 128)])
        parts.append(np.concatenate([high[picked], high[picked], low[picked]], axis=0))
    return np.stack(parts)


def smooth_table():
    bins = np.arange(NF)
    band = (np.abs(bins[:, None] - bins[None, :]) <= SMOOTH).astype(np.float32)
    return np.concatenate([band, np.ones((NF, NF), np.float32)], axis=0).astype(ml_dtypes.bfloat16)


def kernel(
    groups, planes,
    traces, mask_hbm, owners, forward, smoother_hbm, inverse_hbm,
    out,
    mask, tbuf, fbuf, smoother, inverse, maskx, own, big, small, cross_sum, res, packed, rbuf,
    tsem, fsem, send_sem, big_sem, small_sem, rsend, rsem,
):
    wins = traces.shape[0]
    rows = own.shape[3]
    tiles = NF // 128
    pieces = 4 * tiles
    me = lax.axis_index("chan")
    tm = lax.axis_index("tm")
    core = lax.rem(me, 2)
    y = lax.rem(me // 2, 2)
    z = me // 4
    depth = groups // 4
    has_up = z < depth - 1
    has_down = z > 0
    has_big = jnp.where(y == 0, depth - 1 - z, z) > 0
    has_small = jnp.where(y == 0, z, depth - 1 - z) > 0
    big_base = 4 * z - 2 * y
    small_base = 4 * z - 4 + 6 * y

    def channel_start(p):
        return (p % 2) * 64 + ((p // 2) % 2) * 32 + (p // 4) * 16

    def load(p):
        return pltpu.make_async_copy(
            traces.at[:, pl.ds(pl.multiple_of(channel_start(p), 16), 16), :], tbuf.at[p], tsem.at[p]
        )

    tables = [
        pltpu.make_async_copy(source, target, fsem.at[n])
        for n, (source, target) in enumerate(
            ((mask_hbm, mask), (forward, fbuf), (smoother_hbm, smoother), (inverse_hbm, inverse))
        )
    ]
    tables[0].start()
    load(0).start()
    tables[1].start()
    tables[2].start()
    load(1).start()

    barrier = pltpu.get_barrier_semaphore()
    for dz in (-1, 0, 1):
        zz = z + dz

        @pl.when((zz >= 0) & (zz < depth))
        def _():
            for k in range(4):
                for t in range(planes):

                    @pl.when((zz * 4 + k != me) | (t != tm))
                    def _():
                        pl.semaphore_signal(
                            barrier, inc=1, device_id={"chan": zz * 4 + k, "tm": t}, device_id_type=MESH
                        )

    near = 1 + has_up.astype(jnp.int32) + has_down.astype(jnp.int32)
    partners = near * (4 * planes) - 1

    tables[0].wait()
    for w in range(wins):
        row = mask[w : w + 1, :].astype(jnp.float32)
        maskx[w] = jnp.broadcast_to(row, (16, row.shape[1])).astype(jnp.bfloat16)

    def chunk_copies(e, c, q, act, act_local):
        src = own.at[e, c, q]
        slot = (e * 2 + c) * pieces + q
        is_big = e == y
        zt = z + 2 * e - 1
        has_z = (zt >= 0) & (zt < depth)

        def remote(dst, kind, recv, chan):
            act(
                pltpu.make_async_remote_copy(
                    src_ref=src, dst_ref=dst, send_sem=send_sem.at[slot, kind], recv_sem=recv,
                    device_id={"chan": chan}, device_id_type=MESH,
                )
            )

        @pl.when(is_big & has_z)
        def _():
            remote(big.at[q, 4 * (1 - y) + core], 0, big_sem.at[q], zt * 4 + y * 2 + c)

        @pl.when(jnp.logical_not(is_big))
        def _():
            remote(big.at[q, 2 + core], 1, big_sem.at[q], z * 4 + (1 - y) * 2 + c)

        @pl.when(jnp.logical_not(is_big) & has_z)
        def _():
            remote(small.at[q, 2 * (1 - e) + core], 0, small_sem.at[q], zt * 4 + y * 2 + c)

        @pl.when(is_big & (c != core))
        def _():
            remote(big.at[q, 4 * y + core], 2, big_sem.at[q], z * 4 + y * 2 + c)

        @pl.when(jnp.logical_not(is_big) & has_small & (c != core))
        def _():
            remote(small.at[q, 2 * (1 - y) + core], 2, small_sem.at[q], z * 4 + y * 2 + c)

        if act_local:

            @pl.when(is_big & (c == core))
            def _():
                pltpu.make_async_copy(src, big.at[q, 4 * y + core], big_sem.at[q]).start()

            @pl.when(jnp.logical_not(is_big) & has_small & (c == core))
            def _():
                pltpu.make_async_copy(src, small.at[q, 2 * (1 - y) + core], small_sem.at[q]).start()

    def start(copy):
        copy.start()

    def wait_send(copy):
        copy.wait_send()

    tables[1].wait()
    tables[2].wait()
    tables[3].start()

    def produce(p, carry):
        e = lax.rem(p, 2)
        c = lax.rem(p // 2, 2)
        half = p // 4
        load(p).wait()

        @pl.when(p < 6)
        def _():
            load(p + 2).start()

        x = (tbuf[p] * maskx[...]).reshape(wins * 16, tbuf.shape[3])
        spectra = jnp.dot(x, fbuf[...], preferred_element_type=jnp.float32)
        real = spectra[:, :NF]
        imag = spectra[:, NF:]
        amplitude = jnp.sqrt(real * real + imag * imag)
        scaled = amplitude * jnp.float32((2 * SMOOTH + 1) * WATER / NF)
        both = jnp.concatenate([amplitude.astype(jnp.bfloat16), scaled.astype(jnp.bfloat16)], axis=1)
        total = jnp.dot(both, smoother[...], preferred_element_type=jnp.float32)
        gain = jnp.float32(2 * SMOOTH + 1) / (total + jnp.float32((2 * SMOOTH + 1) * EPS))
        for n, part in enumerate((real, imag)):
            white = (part * gain).reshape(wins, 16, NF)
            for h in range(2):
                for f in range(tiles):
                    own[e, c, (2 * half + h) * tiles + f, :, n * 128 : n * 128 + 128] = (
                        white[:, 8 * h : 8 * h + 8, f * 128 : f * 128 + 128]
                        .reshape(wins * 8, 128)
                        .astype(jnp.bfloat16)
                    )

        @pl.when(p == 0)
        def _():
            pl.semaphore_wait(barrier, partners)

        for n in range(AHEAD // 2):
            chunk_copies(e, c, half * (AHEAD // 2) + n, start, True)
        return carry

    lax.fori_loop(0, 8, produce, 0)
    tables[3].wait()

    def cross(buf, q, pairs, first):
        used = sorted({s for pair in pairs for s in pair})

        def step(i, sums):
            r = pl.ds(pl.multiple_of(i * 16, 16), 16)
            re = {s: buf[q, s, r, 0:128].astype(jnp.float32) for s in used}
            im = {s: buf[q, s, r, 128:256].astype(jnp.float32) for s in used}
            new = []
            for n, (a, b) in enumerate(pairs):
                direct = re[a] * re[b] + im[a] * im[b]
                crossed = re[a] * im[b] - im[a] * re[b]
                new.append(sums[2 * n] + (direct[:8] + direct[8:]))
                new.append(sums[2 * n + 1] + (crossed[:8] + crossed[8:]))
            return tuple(new)

        zero = jnp.zeros((8, 128), jnp.float32)
        sums = lax.fori_loop(0, rows // 16, step, (zero,) * (2 * len(pairs)))
        for n in range(len(pairs)):
            cross_sum[first + 8 * n : first + 8 * n + 8, 0:128] = sums[2 * n]
            cross_sum[first + 8 * n : first + 8 * n + 8, 128:256] = sums[2 * n + 1]

    def lags(f):
        value = cross_sum[...]
        high = value.astype(jnp.bfloat16)
        low = (value - high.astype(jnp.float32)).astype(jnp.bfloat16)
        return jnp.dot(
            jnp.concatenate([high, low, high], axis=1), inverse[f], preferred_element_type=jnp.float32
        ).reshape(-1, 8, LAG_PAD)

    def messages(j, base, e, first, listed, act, act_local):
        at = pl.ds(pl.multiple_of(e * 64 + core * 32 + j * 16, 16), 16)
        for k, (s, pair, count, distance) in enumerate(listed):
            chan = base + s
            src = packed.at[j, pl.ds(pair, count)]
            dst = rbuf.at[tm, pl.ds(distance, count), at]
            for t in range(planes):
                mine = (chan == me) & (t == tm)

                @pl.when(jnp.logical_not(mine))
                def _():
                    act(
                        pltpu.make_async_remote_copy(
                            src_ref=src, dst_ref=dst, send_sem=rsend.at[first + k, t], recv_sem=rsem,
                            device_id={"chan": chan, "tm": t}, device_id_type=MESH,
                        )
                    )

                if act_local:

                    @pl.when(mine)
                    def _():
                        pltpu.make_async_copy(src, dst, rsem).start()

    def big_messages(j, act, act_local):
        send = functools.partial(messages, j, big_base, y, 0)

        @pl.when((y == 0) & has_big)
        def _():
            send([(0, 0, 4, 0), (1, 4, 4, 0), (2, 8, 3, 0), (3, 11, 2, 0)], act, act_local)

        @pl.when((y == 0) & jnp.logical_not(has_big))
        def _():
            send([(0, 0, 3, 0), (1, 4, 2, 0), (2, 8, 1, 0)], act, act_local)

        @pl.when((y == 1) & has_big)
        def _():
            send([(0, 1, 3, 1), (1, 4, 4, 0), (2, 8, 3, 0), (3, 11, 2, 0), (4, 13, 1, 0)], act, act_local)

        @pl.when((y == 1) & jnp.logical_not(has_big))
        def _():
            send([(2, 8, 3, 0), (3, 11, 2, 0), (4, 13, 1, 0)], act, act_local)

    def small_messages(j, act, act_local):
        @pl.when(has_small)
        def _():
            messages(j, small_base, 1 - y, 5, [(0, 14, 1, 3), (1, 15, 2, 2)], act, act_local)

    def correlate(q, carry):
        j = q // tiles
        f = lax.rem(q, tiles)

        @pl.when(has_small)
        def _():
            pltpu.make_async_copy(small.at[q], small.at[q], small_sem.at[q]).wait()
            cross(small, q, SMALL, 8 * len(BIG))

        @pl.when(has_big)
        def _():
            pltpu.make_async_copy(big.at[q], big.at[q], big_sem.at[q]).wait()

        @pl.when(jnp.logical_not(has_big))
        def _():
            there = big.at[q, pl.ds(2 * y, 4)]
            pltpu.make_async_copy(there, there, big_sem.at[q]).wait()

        @pl.when(q < pieces - AHEAD)
        def _():
            for c in range(2):
                for e in range(2):
                    chunk_copies(e, c, q + AHEAD, start, True)

        cross(big, q, BIG, 0)

        h = lax.rem(j, 2)

        @pl.when(f == 0)
        def _():
            res[h] = lags(f)

        @pl.when(f > 0)
        def _():
            res[h] += lags(f)

        last = (f == tiles - 1) & (h == 1)

        @pl.when(last & (j > 1))
        def _():
            big_messages(0, wait_send, False)
            small_messages(0, wait_send, False)

        @pl.when(last)
        def _():
            packed[j // 2] = jnp.concatenate([res[0], res[1]], axis=1).astype(jnp.bfloat16)
            big_messages(j // 2, start, True)
            small_messages(j // 2, start, True)

        return carry

    lax.fori_loop(0, pieces, correlate, 0)
    big_messages(1, wait_send, False)
    small_messages(1, wait_send, False)

    def drain(n, carry):
        chunk_copies(n // (2 * pieces), lax.rem(n // pieces, 2), lax.rem(n, pieces), wait_send, False)
        return carry

    lax.fori_loop(0, 4 * pieces, drain, 0)

    valid = jnp.minimum(REACH, groups - 1 - me)
    for n in range(1, REACH + 1):

        @pl.when(valid == n)
        def _():
            whole = rbuf.at[:, pl.ds(0, n)]
            pltpu.make_async_copy(whole, whole, rsem).wait()

    parts = []
    for d in range(REACH):
        total = rbuf[0, d].astype(jnp.float32)
        for t in range(1, planes):
            total = total + rbuf[t, d].astype(jnp.float32)
        parts.append(total.T[:LAGS])
    for p in range(REACH):
        owner = jnp.full(parts[0].shape, owners[0, p], jnp.int32)
        picked = jnp.zeros(parts[0].shape, jnp.float32)
        for d in range(REACH):
            picked = jnp.where(owner == me + (d + 1), parts[d], picked)
        out[:, p, :] = picked


def body(traces, valid_mask, pair_owner):
    _, wins, chans, samples = traces.shape
    groups = lax.axis_size("chan")
    planes = lax.axis_size("tm")
    rows = wins * 8
    tiles = NF // 128
    pieces = 4 * tiles
    vmem = pl.BlockSpec(memory_space=pltpu.VMEM)
    hbm = pl.BlockSpec(memory_space=pl.ANY)
    f32, bf16 = jnp.float32, jnp.bfloat16
    result = pl.pallas_call(
        functools.partial(kernel, groups, planes),
        out_shape=jax.ShapeDtypeStruct((LAGS, REACH, chans), f32),
        in_specs=[hbm, hbm, pl.BlockSpec(memory_space=pltpu.SMEM), hbm, hbm, hbm],
        out_specs=vmem,
        scratch_shapes=[
            pltpu.VMEM((wins, samples), jnp.int32),
            pltpu.VMEM((8, wins, 16, samples), bf16),
            pltpu.VMEM((samples, 2 * NF), bf16),
            pltpu.VMEM((2 * NF, NF), bf16),
            pltpu.VMEM((tiles, 3 * 256, LAG_PAD), bf16),
            pltpu.VMEM((wins, 16, samples), bf16),
            pltpu.VMEM((2, 2, pieces, rows, 256), bf16),
            pltpu.VMEM((pieces, 6, rows, 256), bf16),
            pltpu.VMEM((pieces, 4, rows, 256), bf16),
            pltpu.VMEM(((len(BIG) + len(SMALL)) * 8, 256), f32),
            pltpu.VMEM((2, len(BIG) + len(SMALL), 8, LAG_PAD), f32),
            pltpu.VMEM((2, len(BIG) + len(SMALL), 16, LAG_PAD), bf16),
            pltpu.VMEM((planes, REACH, chans, LAG_PAD), bf16),
            pltpu.SemaphoreType.DMA((8,)),
            pltpu.SemaphoreType.DMA((4,)),
            pltpu.SemaphoreType.DMA((4 * pieces, 3)),
            pltpu.SemaphoreType.DMA((pieces,)),
            pltpu.SemaphoreType.DMA((pieces,)),
            pltpu.SemaphoreType.DMA((7, planes)),
            pltpu.SemaphoreType.DMA,
        ],
        compiler_params=pltpu.CompilerParams(
            collective_id=0, has_side_effects=True, vmem_limit_bytes=56 * 1024 * 1024
        ),
        name="correlate",
    )(
        traces[0],
        valid_mask[0],
        pair_owner,
        jnp.asarray(forward_table(samples)),
        jnp.asarray(smooth_table()),
        jnp.asarray(inverse_table(samples, wins * planes)),
    )
    held = pair_owner[0] >= 0
    result = jnp.where(held[None, :, None], result, jnp.float32(0))
    return result.transpose(1, 0, 2)[None]


def solution(mesh):
    return jax.shard_map(
        body,
        mesh=mesh,
        in_specs=(P("chan", "tm", None, None), P("chan", "tm", None), P("chan", None)),
        out_specs=P("chan", None, None, None),
        check_vma=False,
    )
```

```python
import functools
import math

import jax
import jax.numpy as jnp
import ml_dtypes
import numpy as np
from jax import lax
from jax.experimental import pallas as pl
from jax.experimental.pallas import tpu as pltpu
from jax.sharding import PartitionSpec as P

NF = 256
MAXLAG = 50
LAGS = 2 * MAXLAG + 1
SMOOTH = 4
REACH = 4
LAG_PAD = 128
AHEAD = 4

WATER = 0.05
EPS = 1e-06

MESH = pl.DeviceIdType.MESH

BIG = [
    (0, 1), (0, 2), (0, 3), (0, 4),
    (1, 2), (1, 3), (1, 4), (1, 5),
    (2, 3), (2, 4), (2, 5),
    (3, 4), (3, 5),
    (4, 5),
]
SMALL = [(0, 2), (1, 2), (1, 3)]


def forward_table(samples_count):
    samples = np.arange(samples_count)
    bins = np.arange(1, NF + 1)
    angle = (samples[:, None] * bins[None, :] % samples_count) * (2.0 * math.pi / samples_count)
    return np.concatenate([np.cos(angle), -np.sin(angle)], axis=1).astype(ml_dtypes.bfloat16)


def inverse_table(samples_count, windows_all):
    bins = np.arange(1, NF + 1)
    offsets = np.arange(LAGS) - MAXLAG
    angle = (bins[:, None] * offsets[None, :] % samples_count) * (2.0 * math.pi / samples_count)
    table = np.concatenate([np.cos(angle), -np.sin(angle)], axis=0) / math.sqrt(windows_all * NF)
    table = np.pad(table, ((0, 0), (0, LAG_PAD - LAGS))).astype(np.float32)
    high = table.astype(ml_dtypes.bfloat16)
    low = (table - high.astype(np.float32)).astype(ml_dtypes.bfloat16)
    tiles = NF // 128
    parts = []
    for f in range(tiles):
        picked = np.concatenate([np.arange(f * 128, f * 128 + 128), np.arange(NF + f * 128, NF + f * 128 + 128)])
        parts.append(np.concatenate([high[picked], high[picked], low[picked]], axis=0))
    return np.stack(parts)


def smooth_table():
    bins = np.arange(NF)
    band = (np.abs(bins[:, None] - bins[None, :]) <= SMOOTH).astype(np.float32)
    return np.concatenate([band, np.ones((NF, NF), np.float32)], axis=0).astype(ml_dtypes.bfloat16)


def kernel(
    groups, planes,
    traces, mask_hbm, owners, forward, smoother_hbm, inverse_hbm,
    out,
    mask, tbuf, fbuf, smoother, inverse, maskx, own, big, small, cross_sum, res, packed, rbuf,
    tsem, fsem, send_sem, big_sem, small_sem, rsend, rsem,
):
    wins = traces.shape[0]
    rows = own.shape[3]
    tiles = NF // 128
    pieces = 4 * tiles
    me = lax.axis_index("chan")
    tm = lax.axis_index("tm")
    core = lax.rem(me, 2)
    y = lax.rem(me // 2, 2)
    z = me // 4
    depth = groups // 4
    has_up = z < depth - 1
    has_down = z > 0
    has_big = jnp.where(y == 0, depth - 1 - z, z) > 0
    has_small = jnp.where(y == 0, z, depth - 1 - z) > 0
    big_base = 4 * z - 2 * y
    small_base = 4 * z - 4 + 6 * y

    def channel_start(p):
        return (p % 2) * 64 + ((p // 2) % 2) * 32 + (p // 4) * 16

    def load(p):
        return pltpu.make_async_copy(
            traces.at[:, pl.ds(pl.multiple_of(channel_start(p), 16), 16), :], tbuf.at[p], tsem.at[p]
        )

    tables = [
        pltpu.make_async_copy(source, target, fsem.at[n])
        for n, (source, target) in enumerate(
            ((mask_hbm, mask), (forward, fbuf), (smoother_hbm, smoother), (inverse_hbm, inverse))
        )
    ]
    tables[0].start()
    load(0).start()
    tables[1].start()
    tables[2].start()
    load(1).start()

    barrier = pltpu.get_barrier_semaphore()
    for dz in (-1, 0, 1):
        zz = z + dz

        @pl.when((zz >= 0) & (zz < depth))
        def _():
            for k in range(4):
                for t in range(planes):

                    @pl.when((zz * 4 + k != me) | (t != tm))
                    def _():
                        pl.semaphore_signal(
                            barrier, inc=1, device_id={"chan": zz * 4 + k, "tm": t}, device_id_type=MESH
                        )

    near = 1 + has_up.astype(jnp.int32) + has_down.astype(jnp.int32)
    partners = near * (4 * planes) - 1

    tables[0].wait()
    for w in range(wins):
        row = mask[w : w + 1, :].astype(jnp.float32)
        maskx[w] = jnp.broadcast_to(row, (16, row.shape[1])).astype(jnp.bfloat16)

    def chunk_copies(e, c, q, act, act_local):
        src = own.at[e, c, q]
        slot = (e * 2 + c) * pieces + q
        is_big = e == y
        zt = z + 2 * e - 1
        has_z = (zt >= 0) & (zt < depth)

        def remote(dst, kind, recv, chan):
            act(
                pltpu.make_async_remote_copy(
                    src_ref=src, dst_ref=dst, send_sem=send_sem.at[slot, kind], recv_sem=recv,
                    device_id={"chan": chan}, device_id_type=MESH,
                )
            )

        @pl.when(is_big & has_z)
        def _():
            remote(big.at[q, 4 * (1 - y) + core], 0, big_sem.at[q], zt * 4 + y * 2 + c)

        @pl.when(jnp.logical_not(is_big))
        def _():
            remote(big.at[q, 2 + core], 1, big_sem.at[q], z * 4 + (1 - y) * 2 + c)

        @pl.when(jnp.logical_not(is_big) & has_z)
        def _():
            remote(small.at[q, 2 * (1 - e) + core], 0, small_sem.at[q], zt * 4 + y * 2 + c)

        @pl.when(is_big & (c != core))
        def _():
            remote(big.at[q, 4 * y + core], 2, big_sem.at[q], z * 4 + y * 2 + c)

        @pl.when(jnp.logical_not(is_big) & has_small & (c != core))
        def _():
            remote(small.at[q, 2 * (1 - y) + core], 2, small_sem.at[q], z * 4 + y * 2 + c)

        if act_local:

            @pl.when(is_big & (c == core))
            def _():
                big[q, 4 * y + core] = src[...]

            @pl.when(jnp.logical_not(is_big) & has_small & (c == core))
            def _():
                small[q, 2 * (1 - y) + core] = src[...]

    def start(copy):
        copy.start()

    def wait_send(copy):
        copy.wait_send()

    tables[1].wait()
    tables[2].wait()
    tables[3].start()

    def produce(p, carry):
        e = lax.rem(p, 2)
        c = lax.rem(p // 2, 2)
        half = p // 4
        load(p).wait()

        @pl.when(p < 6)
        def _():
            load(p + 2).start()

        x = (tbuf[p] * maskx[...]).reshape(wins * 16, tbuf.shape[3])
        spectra = jnp.dot(x, fbuf[...], preferred_element_type=jnp.float32)
        real = spectra[:, :NF]
        imag = spectra[:, NF:]
        amplitude = jnp.sqrt(real * real + imag * imag)
        scaled = amplitude * jnp.float32((2 * SMOOTH + 1) * WATER / NF)
        both = jnp.concatenate([amplitude.astype(jnp.bfloat16), scaled.astype(jnp.bfloat16)], axis=1)
        total = jnp.dot(both, smoother[...], preferred_element_type=jnp.float32)
        gain = jnp.float32(2 * SMOOTH + 1) / (total + jnp.float32((2 * SMOOTH + 1) * EPS))
        for n, part in enumerate((real, imag)):
            white = (part * gain).reshape(wins, 16, NF)
            for h in range(2):
                for f in range(tiles):
                    own[e, c, (2 * half + h) * tiles + f, :, n * 128 : n * 128 + 128] = (
                        white[:, 8 * h : 8 * h + 8, f * 128 : f * 128 + 128]
                        .reshape(wins * 8, 128)
                        .astype(jnp.bfloat16)
                    )

        @pl.when(p == 0)
        def _():
            pl.semaphore_wait(barrier, partners)

        for n in range(AHEAD // 2):
            chunk_copies(e, c, half * (AHEAD // 2) + n, start, True)
        return carry

    lax.fori_loop(0, 8, produce, 0)
    tables[3].wait()

    def cross(buf, q, pairs, first):
        used = sorted({s for pair in pairs for s in pair})

        def step(i, sums):
            r = pl.ds(pl.multiple_of(i * 16, 16), 16)
            re = {s: buf[q, s, r, 0:128].astype(jnp.float32) for s in used}
            im = {s: buf[q, s, r, 128:256].astype(jnp.float32) for s in used}
            new = []
            for n, (a, b) in enumerate(pairs):
                direct = re[a] * re[b] + im[a] * im[b]
                crossed = re[a] * im[b] - im[a] * re[b]
                new.append(sums[2 * n] + (direct[:8] + direct[8:]))
                new.append(sums[2 * n + 1] + (crossed[:8] + crossed[8:]))
            return tuple(new)

        zero = jnp.zeros((8, 128), jnp.float32)
        sums = lax.fori_loop(0, rows // 16, step, (zero,) * (2 * len(pairs)))
        for n in range(len(pairs)):
            cross_sum[first + 8 * n : first + 8 * n + 8, 0:128] = sums[2 * n]
            cross_sum[first + 8 * n : first + 8 * n + 8, 128:256] = sums[2 * n + 1]

    def lags(f):
        value = cross_sum[...]
        high = value.astype(jnp.bfloat16)
        low = (value - high.astype(jnp.float32)).astype(jnp.bfloat16)
        return jnp.dot(
            jnp.concatenate([high, low, high], axis=1), inverse[f], preferred_element_type=jnp.float32
        ).reshape(-1, 8, LAG_PAD)

    def messages(j, base, e, first, listed, act, act_local):
        at = pl.ds(pl.multiple_of(e * 64 + core * 32 + j * 16, 16), 16)
        for k, (s, pair, count, distance) in enumerate(listed):
            chan = base + s
            src = packed.at[j, pl.ds(pair, count)]
            dst = rbuf.at[tm, pl.ds(distance, count), at]
            for t in range(planes):
                mine = (chan == me) & (t == tm)

                @pl.when(jnp.logical_not(mine))
                def _():
                    act(
                        pltpu.make_async_remote_copy(
                            src_ref=src, dst_ref=dst, send_sem=rsend.at[first + k, t], recv_sem=rsem,
                            device_id={"chan": chan, "tm": t}, device_id_type=MESH,
                        )
                    )

                if act_local:

                    @pl.when(mine)
                    def _():
                        pltpu.make_async_copy(src, dst, rsem).start()

    def big_messages(j, act, act_local):
        send = functools.partial(messages, j, big_base, y, 0)

        @pl.when((y == 0) & has_big)
        def _():
            send([(0, 0, 4, 0), (1, 4, 4, 0), (2, 8, 3, 0), (3, 11, 2, 0)], act, act_local)

        @pl.when((y == 0) & jnp.logical_not(has_big))
        def _():
            send([(0, 0, 3, 0), (1, 4, 2, 0), (2, 8, 1, 0)], act, act_local)

        @pl.when((y == 1) & has_big)
        def _():
            send([(0, 1, 3, 1), (1, 4, 4, 0), (2, 8, 3, 0), (3, 11, 2, 0), (4, 13, 1, 0)], act, act_local)

        @pl.when((y == 1) & jnp.logical_not(has_big))
        def _():
            send([(2, 8, 3, 0), (3, 11, 2, 0), (4, 13, 1, 0)], act, act_local)

    def small_messages(j, act, act_local):
        @pl.when(has_small)
        def _():
            messages(j, small_base, 1 - y, 5, [(0, 14, 1, 3), (1, 15, 2, 2)], act, act_local)

    def correlate(q, carry):
        j = q // tiles
        f = lax.rem(q, tiles)

        @pl.when(has_small)
        def _():
            there = small.at[q, pl.ds(0, 3)]
            pltpu.make_async_copy(there, there, small_sem.at[q]).wait()
            cross(small, q, SMALL, 8 * len(BIG))

        @pl.when(has_big)
        def _():
            there = big.at[q, pl.ds(0, 5)]
            pltpu.make_async_copy(there, there, big_sem.at[q]).wait()

        @pl.when(jnp.logical_not(has_big))
        def _():
            there = big.at[q, pl.ds(2 * y, 3)]
            pltpu.make_async_copy(there, there, big_sem.at[q]).wait()

        @pl.when(q < pieces - AHEAD)
        def _():
            for c in range(2):
                for e in range(2):
                    chunk_copies(e, c, q + AHEAD, start, True)

        cross(big, q, BIG, 0)

        h = lax.rem(j, 2)

        @pl.when(f == 0)
        def _():
            res[h] = lags(f)

        @pl.when(f > 0)
        def _():
            res[h] += lags(f)

        last = (f == tiles - 1) & (h == 1)

        @pl.when(last & (j > 1))
        def _():
            big_messages(0, wait_send, False)
            small_messages(0, wait_send, False)

        @pl.when(last)
        def _():
            packed[j // 2] = jnp.concatenate([res[0], res[1]], axis=1).astype(jnp.bfloat16)
            big_messages(j // 2, start, True)
            small_messages(j // 2, start, True)

        return carry

    lax.fori_loop(0, pieces, correlate, 0)
    big_messages(1, wait_send, False)
    small_messages(1, wait_send, False)

    def drain(n, carry):
        chunk_copies(n // (2 * pieces), lax.rem(n // pieces, 2), lax.rem(n, pieces), wait_send, False)
        return carry

    lax.fori_loop(0, 4 * pieces, drain, 0)

    valid = jnp.minimum(REACH, groups - 1 - me)
    for n in range(1, REACH + 1):

        @pl.when(valid == n)
        def _():
            whole = rbuf.at[:, pl.ds(0, n)]
            pltpu.make_async_copy(whole, whole, rsem).wait()

    parts = []
    for d in range(REACH):
        total = rbuf[0, d].astype(jnp.float32)
        for t in range(1, planes):
            total = total + rbuf[t, d].astype(jnp.float32)
        parts.append(total.T[:LAGS])
    for p in range(REACH):
        owner = jnp.full(parts[0].shape, owners[0, p], jnp.int32)
        picked = jnp.zeros(parts[0].shape, jnp.float32)
        for d in range(REACH):
            picked = jnp.where(owner == me + (d + 1), parts[d], picked)
        out[pl.ds(p, LAGS, REACH), :] = picked


def body(traces, valid_mask, pair_owner):
    _, wins, chans, samples = traces.shape
    groups = lax.axis_size("chan")
    planes = lax.axis_size("tm")
    rows = wins * 8
    tiles = NF // 128
    pieces = 4 * tiles
    vmem = pl.BlockSpec(memory_space=pltpu.VMEM)
    hbm = pl.BlockSpec(memory_space=pl.ANY)
    f32, bf16 = jnp.float32, jnp.bfloat16
    result = pl.pallas_call(
        functools.partial(kernel, groups, planes),
        out_shape=jax.ShapeDtypeStruct((LAGS * REACH, chans), f32),
        in_specs=[hbm, hbm, pl.BlockSpec(memory_space=pltpu.SMEM), hbm, hbm, hbm],
        out_specs=vmem,
        scratch_shapes=[
            pltpu.VMEM((wins, samples), jnp.int32),
            pltpu.VMEM((8, wins, 16, samples), bf16),
            pltpu.VMEM((samples, 2 * NF), bf16),
            pltpu.VMEM((2 * NF, NF), bf16),
            pltpu.VMEM((tiles, 3 * 256, LAG_PAD), bf16),
            pltpu.VMEM((wins, 16, samples), bf16),
            pltpu.VMEM((2, 2, pieces, rows, 256), bf16),
            pltpu.VMEM((pieces, 6, rows, 256), bf16),
            pltpu.VMEM((pieces, 4, rows, 256), bf16),
            pltpu.VMEM(((len(BIG) + len(SMALL)) * 8, 256), f32),
            pltpu.VMEM((2, len(BIG) + len(SMALL), 8, LAG_PAD), f32),
            pltpu.VMEM((2, len(BIG) + len(SMALL), 16, LAG_PAD), bf16),
            pltpu.VMEM((planes, REACH, chans, LAG_PAD), bf16),
            pltpu.SemaphoreType.DMA((8,)),
            pltpu.SemaphoreType.DMA((4,)),
            pltpu.SemaphoreType.DMA((4 * pieces, 3)),
            pltpu.SemaphoreType.DMA((pieces,)),
            pltpu.SemaphoreType.DMA((pieces,)),
            pltpu.SemaphoreType.DMA((7, planes)),
            pltpu.SemaphoreType.DMA,
        ],
        compiler_params=pltpu.CompilerParams(
            collective_id=0, has_side_effects=True, vmem_limit_bytes=56 * 1024 * 1024
        ),
        name="correlate",
    )(
        traces[0],
        valid_mask[0],
        pair_owner,
        jnp.asarray(forward_table(samples)),
        jnp.asarray(smooth_table()),
        jnp.asarray(inverse_table(samples, wins * planes)),
    )
    return result.reshape(LAGS, REACH, chans).transpose(1, 0, 2)[None]


def solution(mesh):
    return jax.shard_map(
        body,
        mesh=mesh,
        in_specs=(P("chan", "tm", None, None), P("chan", "tm", None), P("chan", None)),
        out_specs=P("chan", None, None, None),
        check_vma=False,
    )
```

```python
import functools
import math

import jax
import jax.numpy as jnp
import ml_dtypes
import numpy as np
from jax import lax
from jax.experimental import pallas as pl
from jax.experimental.pallas import tpu as pltpu
from jax.sharding import PartitionSpec as P

NF = 256
MAXLAG = 50
LAGS = 2 * MAXLAG + 1
SMOOTH = 4
REACH = 4
LAG_PAD = 128
AHEAD = 4

WATER = 0.05
EPS = 1e-06

MESH = pl.DeviceIdType.MESH

BIG = [
    (0, 1), (0, 2), (0, 3), (0, 4),
    (1, 2), (1, 3), (1, 4), (1, 5),
    (2, 3), (2, 4), (2, 5),
    (3, 4), (3, 5),
    (4, 5),
]
SMALL = [(0, 2), (1, 2), (1, 3)]


def forward_table(samples_count):
    samples = np.arange(samples_count)
    bins = np.arange(1, NF + 1)
    angle = (samples[:, None] * bins[None, :] % samples_count) * (2.0 * math.pi / samples_count)
    return np.concatenate([np.cos(angle), -np.sin(angle)], axis=1).astype(ml_dtypes.bfloat16)


def inverse_table(samples_count, windows_all):
    bins = np.arange(1, NF + 1)
    offsets = np.arange(LAGS) - MAXLAG
    angle = (bins[:, None] * offsets[None, :] % samples_count) * (2.0 * math.pi / samples_count)
    table = np.concatenate([np.cos(angle), -np.sin(angle)], axis=0) / math.sqrt(windows_all * NF)
    table = np.pad(table, ((0, 0), (0, LAG_PAD - LAGS))).astype(np.float32)
    high = table.astype(ml_dtypes.bfloat16)
    low = (table - high.astype(np.float32)).astype(ml_dtypes.bfloat16)
    tiles = NF // 128
    parts = []
    for f in range(tiles):
        picked = np.concatenate([np.arange(f * 128, f * 128 + 128), np.arange(NF + f * 128, NF + f * 128 + 128)])
        parts.append(np.concatenate([high[picked], high[picked], low[picked]], axis=0))
    return np.stack(parts)


def smooth_table():
    bins = np.arange(NF)
    band = (np.abs(bins[:, None] - bins[None, :]) <= SMOOTH).astype(np.float32)
    return np.concatenate([band, np.ones((NF, NF), np.float32)], axis=0).astype(ml_dtypes.bfloat16)


def kernel(
    groups, planes,
    traces, mask_hbm, owners, forward, smoother_hbm, inverse_hbm,
    out,
    mask, tbuf, fbuf, smoother, inverse, maskx, own, big, small, cross_sum, res, packed, rbuf,
    tsem, fsem, send_sem, big_sem, small_sem, rsend, rsem,
):
    wins = traces.shape[0]
    rows = own.shape[3]
    tiles = NF // 128
    pieces = 4 * tiles
    me = lax.axis_index("chan")
    tm = lax.axis_index("tm")
    core = lax.rem(me, 2)
    y = lax.rem(me // 2, 2)
    z = me // 4
    depth = groups // 4
    has_up = z < depth - 1
    has_down = z > 0
    has_big = jnp.where(y == 0, depth - 1 - z, z) > 0
    has_small = jnp.where(y == 0, z, depth - 1 - z) > 0
    big_base = 4 * z - 2 * y
    small_base = 4 * z - 4 + 6 * y

    def channel_start(p):
        return (p % 2) * 64 + lax.rem(p // 2 + core, 2) * 32 + (p // 4) * 16

    def load(p):
        return pltpu.make_async_copy(
            traces.at[:, pl.ds(pl.multiple_of(channel_start(p), 16), 16), :], tbuf.at[p], tsem.at[p]
        )

    tables = [
        pltpu.make_async_copy(source, target, fsem.at[n])
        for n, (source, target) in enumerate(
            ((mask_hbm, mask), (forward, fbuf), (smoother_hbm, smoother), (inverse_hbm, inverse))
        )
    ]
    tables[0].start()
    load(0).start()
    tables[1].start()
    tables[2].start()
    load(1).start()

    barrier = pltpu.get_barrier_semaphore()
    for dz in (-1, 0, 1):
        zz = z + dz

        @pl.when((zz >= 0) & (zz < depth))
        def _():
            for k in range(4):
                for t in range(planes):

                    @pl.when((zz * 4 + k != me) | (t != tm))
                    def _():
                        pl.semaphore_signal(
                            barrier, inc=1, device_id={"chan": zz * 4 + k, "tm": t}, device_id_type=MESH
                        )

    near = 1 + has_up.astype(jnp.int32) + has_down.astype(jnp.int32)
    partners = near * (4 * planes) - 1

    tables[0].wait()
    for w in range(wins):
        row = mask[w : w + 1, :].astype(jnp.float32)
        maskx[w] = jnp.broadcast_to(row, (16, row.shape[1])).astype(jnp.bfloat16)

    def chunk_copies(e, c, q, act, act_local):
        src = own.at[e, c, q]
        slot = (e * 2 + c) * pieces + q
        is_big = e == y
        zt = z + 2 * e - 1
        has_z = (zt >= 0) & (zt < depth)

        def remote(dst, kind, recv, chan):
            act(
                pltpu.make_async_remote_copy(
                    src_ref=src, dst_ref=dst, send_sem=send_sem.at[slot, kind], recv_sem=recv,
                    device_id={"chan": chan}, device_id_type=MESH,
                )
            )

        @pl.when(is_big & has_z)
        def _():
            remote(big.at[q, 4 * (1 - y) + core], 0, big_sem.at[q], zt * 4 + y * 2 + c)

        @pl.when(jnp.logical_not(is_big))
        def _():
            remote(big.at[q, 2 + core], 1, big_sem.at[q], z * 4 + (1 - y) * 2 + c)

        @pl.when(jnp.logical_not(is_big) & has_z)
        def _():
            remote(small.at[q, 2 * (1 - e) + core], 0, small_sem.at[q], zt * 4 + y * 2 + c)

        @pl.when(is_big & (c != core))
        def _():
            remote(big.at[q, 4 * y + core], 2, big_sem.at[q], z * 4 + y * 2 + c)

        @pl.when(jnp.logical_not(is_big) & has_small & (c != core))
        def _():
            remote(small.at[q, 2 * (1 - y) + core], 2, small_sem.at[q], z * 4 + y * 2 + c)

        if act_local:

            @pl.when(is_big & (c == core))
            def _():
                big[q, 4 * y + core] = src[...]

            @pl.when(jnp.logical_not(is_big) & has_small & (c == core))
            def _():
                small[q, 2 * (1 - y) + core] = src[...]

    def start(copy):
        copy.start()

    def wait_send(copy):
        copy.wait_send()

    tables[1].wait()
    tables[2].wait()
    tables[3].start()

    def produce(p, carry):
        e = lax.rem(p, 2)
        c = lax.rem(p // 2 + core, 2)
        half = p // 4
        load(p).wait()

        @pl.when(p < 6)
        def _():
            load(p + 2).start()

        x = (tbuf[p] * maskx[...]).reshape(wins * 16, tbuf.shape[3])
        spectra = jnp.dot(x, fbuf[...], preferred_element_type=jnp.float32)
        real = spectra[:, :NF]
        imag = spectra[:, NF:]
        amplitude = jnp.sqrt(real * real + imag * imag)
        scaled = amplitude * jnp.float32((2 * SMOOTH + 1) * WATER / NF)
        both = jnp.concatenate([amplitude.astype(jnp.bfloat16), scaled.astype(jnp.bfloat16)], axis=1)
        total = jnp.dot(both, smoother[...], preferred_element_type=jnp.float32)
        gain = jnp.float32(2 * SMOOTH + 1) / (total + jnp.float32((2 * SMOOTH + 1) * EPS))
        for n, part in enumerate((real, imag)):
            white = (part * gain).reshape(wins, 16, NF)
            for h in range(2):
                for f in range(tiles):
                    own[e, c, (2 * half + h) * tiles + f, :, n * 128 : n * 128 + 128] = (
                        white[:, 8 * h : 8 * h + 8, f * 128 : f * 128 + 128]
                        .reshape(wins * 8, 128)
                        .astype(jnp.bfloat16)
                    )

        @pl.when(p == 0)
        def _():
            pl.semaphore_wait(barrier, partners)

        for n in range(AHEAD // 2):
            chunk_copies(e, c, half * (AHEAD // 2) + n, start, True)
        return carry

    lax.fori_loop(0, 8, produce, 0)
    tables[3].wait()

    def cross(buf, q, pairs, first):
        used = sorted({s for pair in pairs for s in pair})

        def step(i, sums):
            r = pl.ds(pl.multiple_of(i * 16, 16), 16)
            re = {s: buf[q, s, r, 0:128].astype(jnp.float32) for s in used}
            im = {s: buf[q, s, r, 128:256].astype(jnp.float32) for s in used}
            new = []
            for n, (a, b) in enumerate(pairs):
                direct = re[a] * re[b] + im[a] * im[b]
                crossed = re[a] * im[b] - im[a] * re[b]
                new.append(sums[2 * n] + (direct[:8] + direct[8:]))
                new.append(sums[2 * n + 1] + (crossed[:8] + crossed[8:]))
            return tuple(new)

        zero = jnp.zeros((8, 128), jnp.float32)
        sums = lax.fori_loop(0, rows // 16, step, (zero,) * (2 * len(pairs)))
        for n in range(len(pairs)):
            cross_sum[first + 8 * n : first + 8 * n + 8, 0:128] = sums[2 * n]
            cross_sum[first + 8 * n : first + 8 * n + 8, 128:256] = sums[2 * n + 1]

    def lags(f):
        value = cross_sum[...]
        high = value.astype(jnp.bfloat16)
        low = (value - high.astype(jnp.float32)).astype(jnp.bfloat16)
        return jnp.dot(
            jnp.concatenate([high, low, high], axis=1), inverse[f], preferred_element_type=jnp.float32
        ).reshape(-1, 8, LAG_PAD)

    def messages(j, base, e, first, listed, act, act_local):
        at = pl.ds(pl.multiple_of(e * 64 + core * 32 + j * 16, 16), 16)
        for k, (s, pair, count, distance) in enumerate(listed):
            chan = base + s
            src = packed.at[j, pl.ds(pair, count)]
            dst = rbuf.at[tm, pl.ds(distance, count), at]
            for t in range(planes):
                mine = (chan == me) & (t == tm)

                @pl.when(jnp.logical_not(mine))
                def _():
                    act(
                        pltpu.make_async_remote_copy(
                            src_ref=src, dst_ref=dst, send_sem=rsend.at[first + k, t], recv_sem=rsem,
                            device_id={"chan": chan, "tm": t}, device_id_type=MESH,
                        )
                    )

                if act_local:

                    @pl.when(mine)
                    def _():
                        pltpu.make_async_copy(src, dst, rsem).start()

    def big_messages(j, act, act_local):
        send = functools.partial(messages, j, big_base, y, 0)

        @pl.when((y == 0) & has_big)
        def _():
            send([(0, 0, 4, 0), (1, 4, 4, 0), (2, 8, 3, 0), (3, 11, 2, 0)], act, act_local)

        @pl.when((y == 0) & jnp.logical_not(has_big))
        def _():
            send([(0, 0, 3, 0), (1, 4, 2, 0), (2, 8, 1, 0)], act, act_local)

        @pl.when((y == 1) & has_big)
        def _():
            send([(0, 1, 3, 1), (1, 4, 4, 0), (2, 8, 3, 0), (3, 11, 2, 0), (4, 13, 1, 0)], act, act_local)

        @pl.when((y == 1) & jnp.logical_not(has_big))
        def _():
            send([(2, 8, 3, 0), (3, 11, 2, 0), (4, 13, 1, 0)], act, act_local)

    def small_messages(j, act, act_local):
        @pl.when(has_small)
        def _():
            messages(j, small_base, 1 - y, 5, [(0, 14, 1, 3), (1, 15, 2, 2)], act, act_local)

    def correlate(q, carry):
        j = q // tiles
        f = lax.rem(q, tiles)

        @pl.when(has_small)
        def _():
            there = small.at[q, pl.ds(0, 3)]
            pltpu.make_async_copy(there, there, small_sem.at[q]).wait()
            cross(small, q, SMALL, 8 * len(BIG))

        @pl.when(has_big)
        def _():
            there = big.at[q, pl.ds(0, 5)]
            pltpu.make_async_copy(there, there, big_sem.at[q]).wait()

        @pl.when(jnp.logical_not(has_big))
        def _():
            there = big.at[q, pl.ds(2 * y, 3)]
            pltpu.make_async_copy(there, there, big_sem.at[q]).wait()

        @pl.when(q < pieces - AHEAD)
        def _():
            for c in range(2):
                for e in range(2):
                    chunk_copies(e, lax.rem(c + core, 2), q + AHEAD, start, True)

        cross(big, q, BIG, 0)

        h = lax.rem(j, 2)

        @pl.when(f == 0)
        def _():
            res[h] = lags(f)

        @pl.when(f > 0)
        def _():
            res[h] += lags(f)

        last = (f == tiles - 1) & (h == 1)

        @pl.when(last & (j > 1))
        def _():
            big_messages(0, wait_send, False)
            small_messages(0, wait_send, False)

        @pl.when(last)
        def _():
            packed[j // 2] = jnp.concatenate([res[0], res[1]], axis=1).astype(jnp.bfloat16)
            big_messages(j // 2, start, True)
            small_messages(j // 2, start, True)

        return carry

    lax.fori_loop(0, pieces, correlate, 0)
    big_messages(1, wait_send, False)
    small_messages(1, wait_send, False)

    def drain(n, carry):
        chunk_copies(n // (2 * pieces), lax.rem(n // pieces, 2), lax.rem(n, pieces), wait_send, False)
        return carry

    lax.fori_loop(0, 4 * pieces, drain, 0)

    valid = jnp.minimum(REACH, groups - 1 - me)
    for n in range(1, REACH + 1):

        @pl.when(valid == n)
        def _():
            whole = rbuf.at[:, pl.ds(0, n)]
            pltpu.make_async_copy(whole, whole, rsem).wait()

    parts = []
    for d in range(REACH):
        total = rbuf[0, d].astype(jnp.float32)
        for t in range(1, planes):
            total = total + rbuf[t, d].astype(jnp.float32)
        parts.append(total.T[:LAGS])
    for p in range(REACH):
        owner = jnp.full(parts[0].shape, owners[0, p], jnp.int32)
        picked = jnp.zeros(parts[0].shape, jnp.float32)
        for d in range(REACH):
            picked = jnp.where(owner == me + (d + 1), parts[d], picked)
        out[pl.ds(p, LAGS, REACH), :] = picked


def body(traces, valid_mask, pair_owner):
    _, wins, chans, samples = traces.shape
    groups = lax.axis_size("chan")
    planes = lax.axis_size("tm")
    rows = wins * 8
    tiles = NF // 128
    pieces = 4 * tiles
    vmem = pl.BlockSpec(memory_space=pltpu.VMEM)
    hbm = pl.BlockSpec(memory_space=pl.ANY)
    f32, bf16 = jnp.float32, jnp.bfloat16
    result = pl.pallas_call(
        functools.partial(kernel, groups, planes),
        out_shape=jax.ShapeDtypeStruct((LAGS * REACH, chans), f32),
        in_specs=[hbm, hbm, pl.BlockSpec(memory_space=pltpu.SMEM), hbm, hbm, hbm],
        out_specs=vmem,
        scratch_shapes=[
            pltpu.VMEM((wins, samples), jnp.int32),
            pltpu.VMEM((8, wins, 16, samples), bf16),
            pltpu.VMEM((samples, 2 * NF), bf16),
            pltpu.VMEM((2 * NF, NF), bf16),
            pltpu.VMEM((tiles, 3 * 256, LAG_PAD), bf16),
            pltpu.VMEM((wins, 16, samples), bf16),
            pltpu.VMEM((2, 2, pieces, rows, 256), bf16),
            pltpu.VMEM((pieces, 6, rows, 256), bf16),
            pltpu.VMEM((pieces, 4, rows, 256), bf16),
            pltpu.VMEM(((len(BIG) + len(SMALL)) * 8, 256), f32),
            pltpu.VMEM((2, len(BIG) + len(SMALL), 8, LAG_PAD), f32),
            pltpu.VMEM((2, len(BIG) + len(SMALL), 16, LAG_PAD), bf16),
            pltpu.VMEM((planes, REACH, chans, LAG_PAD), bf16),
            pltpu.SemaphoreType.DMA((8,)),
            pltpu.SemaphoreType.DMA((4,)),
            pltpu.SemaphoreType.DMA((4 * pieces, 3)),
            pltpu.SemaphoreType.DMA((pieces,)),
            pltpu.SemaphoreType.DMA((pieces,)),
            pltpu.SemaphoreType.DMA((7, planes)),
            pltpu.SemaphoreType.DMA,
        ],
        compiler_params=pltpu.CompilerParams(
            collective_id=0, has_side_effects=True, vmem_limit_bytes=56 * 1024 * 1024
        ),
        name="correlate",
    )(
        traces[0],
        valid_mask[0],
        pair_owner,
        jnp.asarray(forward_table(samples)),
        jnp.asarray(smooth_table()),
        jnp.asarray(inverse_table(samples, wins * planes)),
    )
    return result.reshape(LAGS, REACH, chans).transpose(1, 0, 2)[None]


def solution(mesh):
    return jax.shard_map(
        body,
        mesh=mesh,
        in_specs=(P("chan", "tm", None, None), P("chan", "tm", None), P("chan", None)),
        out_specs=P("chan", None, None, None),
        check_vma=False,
    )
```
